32 devices in a mesh: ctx: 16 (over z, y, core), tp: 2 (over x).
Axes of the slice: x: 2, y: 2, z: 4, core: 2. Of those that a mesh axis runs over, the one named last changes fastest.
Arguments:
- queries: bfloat16 [4096, 2048], P('ctx', 'tp'), may hold values from -5 to 5
- keys: bfloat16 [4096, 256], P('ctx', 'tp'), may hold values from -5 to 5
- values: bfloat16 [4096, 256], P('ctx', 'tp'), may hold values from -6 to 6
- out_weight: bfloat16 [2048, 4096], P('tp'), may hold values from -0.125 to 0.125
- cotangent: bfloat16 [4096, 4096], P('ctx', 'tp'), may hold values from -6 to 6
- doc_lengths: int32 [8], replicated, may hold values from 1 to 2048, 4096 in all
Outputs:
- mixed_out: bfloat16 [4096, 4096], P('ctx', 'tp')
- query_grad: bfloat16 [4096, 2048], P('ctx', 'tp')
- keys_gradient: bfloat16 [4096, 256], P('ctx', 'tp')
- values_gradient: bfloat16 [4096, 256], P('ctx', 'tp')
The draws below stay inside these ranges and needn't reach their ends.
Inputs may be any that keep to these rules, and one draw needn't show every extreme that they name: `doc_lengths`: document lengths in order along the packed sequence; they sum to 4096 and the longest is exactly 2048.
All inputs are finite; a program needn't handle non-finite values.
Results may differ from the reference program's by a relative error of at most 0.022.
Values may be sent and summed in bfloat16 or wider, within the bound.
No kernel may reach another device: no remote copies, remote signals or barrier semaphores. Data moves between devices by JAX's collectives and lax.ppermute only.
A program may use at most 192 MiB of HBM per device.

```python
import math
import jax
import jax.numpy as jnp
import numpy as np
from jax import lax

D = 4096
QUERY_HEADS = 16
KEY_VALUE_HEADS = 2
HEAD_WIDTH = 128
SHARD_TOKENS = 256
REACH = 8
PACKED_TOKENS = 4096
DOC_MOST = 2048
DOCS = 8


def draw_queries(key, part):
    local_keys = jax.random.fold_in(key, 11)
    sampled_inputs = jax.random.truncated_normal(local_keys, -4.0, 4.0, (PACKED_TOKENS, QUERY_HEADS, HEAD_WIDTH), jnp.float32)
    return sampled_inputs.reshape(PACKED_TOKENS, QUERY_HEADS * HEAD_WIDTH).astype(jnp.bfloat16)


def draw_keys(key, part):
    local_keys = jax.random.fold_in(key, 13)
    sampled_inputs = jax.random.truncated_normal(local_keys, -4.0, 4.0, (PACKED_TOKENS, KEY_VALUE_HEADS, HEAD_WIDTH), jnp.float32)
    return sampled_inputs.reshape(PACKED_TOKENS, KEY_VALUE_HEADS * HEAD_WIDTH).astype(jnp.bfloat16)


def level_of(own_key, shape, shards, low, top_value):
    level = 1.0
    for dim, blocks in shards:
        heights = jax.random.uniform(jax.random.fold_in(jax.random.fold_in(own_key, 6), dim), (blocks,), jnp.float32, low / len(shards), top_value / len(shards))
        level = level * jnp.repeat(jnp.exp(heights), shape[dim] // blocks).reshape((-1,) + (1,) * (len(shape) - 1 - dim))
    return level


def profile(count, total, reach, slope):
    loads = [(1 << 20) // math.isqrt(grade ** slope) + 1 for grade in range(2, count + 1)]
    rest, counts = total - reach - (count - 1), [1] * (count - 1)
    while rest > 0:
        movable = [i for i in range(count - 1) if counts[i] < reach]
        whole, remaining = sum([loads[i] for i in movable]), rest
        for i in movable:
            addition = min(reach - counts[i], max(1, remaining * loads[i] // whole), rest)
            counts[i] = counts[i] + addition
            rest = rest - addition
    return np.array([reach] + counts)


def uneven(stream_key, number_of, total, limit, lean):
    if number_of == 2:
        one = jax.random.randint(stream_key, (), max(1, total - limit), min(limit, total - 1) + 1)
        return jnp.stack([one, total - one])
    tallies = jnp.asarray(profile(number_of, total, limit, lean), jnp.int32)
    twos = (number_of - 1) // 2
    donor, receiver = tallies[1:1 + 2 * twos:2], tallies[2:2 + 2 * twos:2]
    margin = jnp.minimum(donor - 1, limit - receiver)
    moved = jax.random.randint(jax.random.fold_in(stream_key, 1), (twos,), 0, 1 << 20) % (margin + 1)
    tallies = tallies.at[1:1 + 2 * twos:2].set(donor - moved).at[2:2 + 2 * twos:2].set(receiver + moved)
    return tallies[jax.random.permutation(jax.random.fold_in(stream_key, 2), number_of)]


def gaussian(stream_key, shape, deviation, most, cuts=(), kind=jnp.bfloat16):
    entries = jax.random.normal(stream_key, shape, jnp.float32) * deviation
    if len(cuts) > 0:
        entries = level_of(stream_key, shape, cuts, -0.22, 0.18) * entries
    return jnp.clip(entries, min=-most, max=most).astype(kind)


def setup_inputs(seed: int = 0) -> dict:
    key_list = jax.random.split(jax.random.key(seed), 7)
    return {
        "queries": draw_queries(jax.random.fold_in(key_list[6], 71), 0),
        "keys": draw_keys(jax.random.fold_in(key_list[6], 71), 0),
        "values": gaussian(key_list[2], (PACKED_TOKENS, KEY_VALUE_HEADS * HEAD_WIDTH), 1.0, 6.0, ((0, 16), (1, 2))),
        "out_weight": gaussian(key_list[3], (QUERY_HEADS * HEAD_WIDTH, D), (QUERY_HEADS * HEAD_WIDTH) ** -0.5, 0.125, ((0, 2),)),
        "cotangent": gaussian(key_list[4], (PACKED_TOKENS, D), 1.0, 6.0, ((0, 16), (1, 2))),
        "doc_lengths": uneven(key_list[5], DOCS, PACKED_TOKENS, DOC_MOST, 2).astype(jnp.int32),
    }


def reference(queries, keys, values, out_weight, cotangent, doc_lengths):
    group_width = QUERY_HEADS // KEY_VALUE_HEADS
    score_scale = 1.0 / math.sqrt(HEAD_WIDTH)
    head_window = REACH * SHARD_TOKENS
    span_rows = head_window + SHARD_TOKENS
    block_count = PACKED_TOKENS // SHARD_TOKENS
    doc_ends = jnp.cumsum(doc_lengths).astype(jnp.int32)
    positions = jnp.arange(PACKED_TOKENS, dtype=jnp.int32)
    segments = lax.optimization_barrier(jnp.sum((positions[:, None] >= doc_ends[None, :]).astype(jnp.int32), axis=1)).astype(jnp.int32)
    pad_seg = jnp.concatenate([jnp.full((head_window,), -1, jnp.int32), segments])
    every_query = queries.reshape(PACKED_TOKENS, KEY_VALUE_HEADS, group_width, HEAD_WIDTH)
    padded_keys = jnp.concatenate([jnp.zeros((head_window, KEY_VALUE_HEADS * HEAD_WIDTH), keys.dtype), keys]).reshape(PACKED_TOKENS + head_window, KEY_VALUE_HEADS, HEAD_WIDTH)
    padded_values = jnp.concatenate([jnp.zeros((head_window, KEY_VALUE_HEADS * HEAD_WIDTH), values.dtype), values]).reshape(PACKED_TOKENS + head_window, KEY_VALUE_HEADS, HEAD_WIDTH)
    local_offsets = jnp.arange(SHARD_TOKENS, dtype=jnp.int32)
    span_offsets = jnp.arange(span_rows, dtype=jnp.int32)

    def block_parts(block_id):
        first_row = (block_id * SHARD_TOKENS).astype(jnp.int32)
        query_blk = lax.dynamic_slice_in_dim(every_query, first_row, SHARD_TOKENS, 0).astype(jnp.float32)
        key_blk = lax.dynamic_slice_in_dim(padded_keys, first_row, span_rows, 0).astype(jnp.float32)
        value_blk = lax.dynamic_slice_in_dim(padded_values, first_row, span_rows, 0).astype(jnp.float32)
        query_seg = lax.dynamic_slice_in_dim(segments, first_row, SHARD_TOKENS, 0)
        key_seg = lax.dynamic_slice_in_dim(pad_seg, first_row, span_rows, 0)
        query_pos = first_row + local_offsets
        key_pos = first_row - head_window + span_offsets
        allowed = (query_seg[:, None] == key_seg[None, :]) & (key_pos[None, :] <= query_pos[:, None])
        scores = jnp.einsum('pkgd,jkd->kgpj', query_blk, key_blk) * score_scale
        return (query_blk, key_blk, value_blk, allowed, scores)

    def forward_block(block_id):
        query_blk, key_blk, value_blk, allowed, scores = block_parts(block_id)
        row_max = lax.optimization_barrier(jnp.max(jnp.where(allowed, scores, -jnp.inf), axis=-1, keepdims=True))
        row_mass = lax.optimization_barrier(jnp.sum(jnp.where(allowed, jnp.exp(scores - row_max), 0.0), axis=-1, keepdims=True))
        log_mass = row_max + jnp.log(row_mass)
        prob_low = lax.optimization_barrier(jnp.where(allowed, jnp.exp(scores - log_mass), 0.0).astype(jnp.bfloat16)).astype(jnp.float32)
        output = jnp.einsum('kgpj,jkd->pkgd', prob_low, value_blk)
        return (output.astype(jnp.bfloat16).reshape(SHARD_TOKENS, QUERY_HEADS * HEAD_WIDTH), log_mass)
    block_ids = jnp.arange(block_count, dtype=jnp.int32)
    grouped_attention, log_masses = lax.map(forward_block, block_ids)
    grouped_attention = grouped_attention.reshape(PACKED_TOKENS, QUERY_HEADS * HEAD_WIDTH)
    half_cols = QUERY_HEADS * HEAD_WIDTH // 2
    first_half = jnp.dot(grouped_attention[:, :half_cols], out_weight[:half_cols], preferred_element_type=jnp.float32).astype(jnp.bfloat16)
    second_half = jnp.dot(grouped_attention[:, half_cols:], out_weight[half_cols:], preferred_element_type=jnp.float32).astype(jnp.bfloat16)
    first_half = lax.optimization_barrier(first_half)
    second_half = lax.optimization_barrier(second_half)
    mixed_out = (first_half.astype(jnp.float32) + second_half.astype(jnp.float32)).astype(jnp.bfloat16)
    attention_gradient = lax.dot_general(cotangent, out_weight, (((1,), (1,)), ((), ())), preferred_element_type=jnp.float32).astype(jnp.bfloat16)
    attention_gradient = lax.optimization_barrier(attention_gradient)
    row_delta_terms = lax.optimization_barrier(jnp.sum((attention_gradient.astype(jnp.float32) * grouped_attention.astype(jnp.float32)).reshape(PACKED_TOKENS, KEY_VALUE_HEADS, group_width, HEAD_WIDTH), axis=-1))

    def backward_block(carry, block_id):
        key_gradient_total, value_gradient_total = carry
        query_blk, key_blk, value_blk, allowed, scores = block_parts(block_id)
        first_row = (block_id * SHARD_TOKENS).astype(jnp.int32)
        prob_full = jnp.where(allowed, jnp.exp(scores - log_masses[block_id]), 0.0)
        prob_low = lax.optimization_barrier(prob_full.astype(jnp.bfloat16)).astype(jnp.float32)
        block_gradient = lax.dynamic_slice_in_dim(attention_gradient, first_row, SHARD_TOKENS, 0).reshape(SHARD_TOKENS, KEY_VALUE_HEADS, group_width, HEAD_WIDTH).astype(jnp.float32)
        delta_blk = jnp.transpose(lax.dynamic_slice_in_dim(row_delta_terms, first_row, SHARD_TOKENS, 0), (1, 2, 0))[..., None]
        grad_prob = jnp.einsum('pkgd,jkd->kgpj', block_gradient, value_blk)
        grad_score = lax.optimization_barrier((prob_full * (grad_prob - delta_blk)).astype(jnp.bfloat16)).astype(jnp.float32)
        query_part = jnp.einsum('kgpj,jkd->pkgd', grad_score, key_blk) * score_scale
        key_part = jnp.einsum('kgpj,pkgd->jkd', grad_score, query_blk) * score_scale
        value_part = jnp.einsum('kgpj,pkgd->jkd', prob_low, block_gradient)
        key_gradient_total = lax.dynamic_update_slice_in_dim(key_gradient_total, lax.dynamic_slice_in_dim(key_gradient_total, first_row, span_rows, 0) + key_part, first_row, 0)
        value_gradient_total = lax.dynamic_update_slice_in_dim(value_gradient_total, lax.dynamic_slice_in_dim(value_gradient_total, first_row, span_rows, 0) + value_part, first_row, 0)
        return ((key_gradient_total, value_gradient_total), query_part.astype(jnp.bfloat16).reshape(SHARD_TOKENS, QUERY_HEADS * HEAD_WIDTH))
    initial_totals = (jnp.zeros((PACKED_TOKENS + head_window, KEY_VALUE_HEADS, HEAD_WIDTH), jnp.float32), jnp.zeros((PACKED_TOKENS + head_window, KEY_VALUE_HEADS, HEAD_WIDTH), jnp.float32))
    (key_gradient_total, value_gradient_total), query_grad = lax.scan(backward_block, initial_totals, block_ids)
    query_grad = query_grad.reshape(PACKED_TOKENS, QUERY_HEADS * HEAD_WIDTH)
    keys_gradient = key_gradient_total[head_window:].reshape(PACKED_TOKENS, KEY_VALUE_HEADS * HEAD_WIDTH).astype(jnp.bfloat16)
    values_gradient = value_gradient_total[head_window:].reshape(PACKED_TOKENS, KEY_VALUE_HEADS * HEAD_WIDTH).astype(jnp.bfloat16)
    return (mixed_out, query_grad, keys_gradient, values_gradient)
```

```python
from functools import partial
import math

import jax
import jax.numpy as jnp
from jax import lax
from jax.experimental import pallas as pl
from jax.experimental.pallas import tpu as pltpu
from jax.sharding import PartitionSpec as P

HEAD_WIDTH = 128
REACH = 8
GROUP = 4
BACK = REACH // GROUP
PLANES = BACK + 1
WINDOW = PLANES * GROUP
LOG2_E = math.log2(math.e)
MASKED = -1e30
NT = (((1,), (1,)), ((), ()))


def shifted(block, distance):
    size = lax.axis_size("ctx")
    route = [(i, i + distance) for i in range(size) if 0 <= i + distance < size]
    return lax.ppermute(block, "ctx", route)


def swapped(block, bit):
    return lax.ppermute(block, "ctx", [(i, i ^ bit) for i in range(lax.axis_size("ctx"))])


def tp_swapped(block):
    return lax.ppermute(block, "tp", [(0, 1), (1, 0)])


def params(mebibytes):
    return pltpu.CompilerParams(vmem_limit_bytes=mebibytes * 2**20)


def window_slot(block, place):
    plane = BACK - block // GROUP
    half = (block // 2 + place // 2) % 2
    core = (block + place) % 2
    return core, half * PLANES + plane


def doc_rows(lens_ref, first, rows):
    positions = first + lax.broadcasted_iota(jnp.int32, (1, rows), 1)

    def add_doc(doc, carry):
        end, starts, start = carry
        length = lens_ref[doc]
        end = end + length
        return (
            end,
            starts + jnp.where(positions >= end, length, 0),
            start + jnp.where(first >= end, length, 0),
        )

    zero = jnp.int32(0)
    _, starts, start = lax.fori_loop(
        0, lens_ref.shape[0], add_doc, (zero, jnp.zeros((1, rows), jnp.int32), zero)
    )
    return positions, starts, start


def block_bias(block, base, rows, positions, starts):
    key_pos = base + block * rows + lax.broadcasted_iota(jnp.int32, (rows, rows), 0)
    return jnp.where((key_pos >= starts) & (key_pos <= positions), 0.0, MASKED).astype(jnp.float32)


def head(h):
    return slice(h * HEAD_WIDTH, (h + 1) * HEAD_WIDTH)


def window_place(rows):
    device = lax.axis_index("ctx")
    place = device % GROUP
    first = device * rows
    base = first - (BACK * GROUP + place) * rows
    return place, first, base


def forward_kernel(heads, lens_ref, q_ref, *rest):
    parts = rest[: 4 * PLANES * 2]
    out_ref, mass_ref, win_ref, acc_ref, max_ref, sum_ref = rest[4 * PLANES * 2 :]
    rows = q_ref.shape[0]
    scale = LOG2_E / math.sqrt(HEAD_WIDTH)
    place, first, base = window_place(rows)
    positions, starts, start = doc_rows(lens_ref, first, rows)
    for core in range(2):
        for slot in range(2 * PLANES):
            plane, half = slot % PLANES, slot // PLANES
            where = (BACK - plane) * GROUP + (place ^ (half * 2 + core))
            for kind in range(2):
                win_ref[where, kind] = parts[(core * 2 * PLANES + slot) * 2 + kind][...]
    acc_ref[...] = jnp.zeros_like(acc_ref)
    max_ref[...] = jnp.full_like(max_ref, MASKED)
    sum_ref[...] = jnp.zeros_like(sum_ref)

    def visit(block, carry):
        keys = win_ref[block, 0]
        values_t = win_ref[block, 1].T
        bias = block_bias(block, base, rows, positions, starts)
        for h in range(heads):
            scores = (
                lax.dot_general(keys, q_ref[:, head(h)], NT, preferred_element_type=jnp.float32)
                * scale
                + bias
            )
            old_max = max_ref[h : h + 1, :]
            new_max = jnp.maximum(old_max, jnp.max(scores, axis=0, keepdims=True))
            prob = jnp.exp2(scores - new_max)
            alpha = jnp.exp2(old_max - new_max)
            max_ref[h : h + 1, :] = new_max
            sum_ref[h : h + 1, :] = sum_ref[h : h + 1, :] * alpha + jnp.sum(
                prob, axis=0, keepdims=True
            )
            acc_ref[h] = acc_ref[h] * alpha + jnp.dot(
                values_t, prob.astype(jnp.bfloat16), preferred_element_type=jnp.float32
            )
        return carry

    lax.fori_loop((start - base) // rows, BACK * GROUP + place + 1, visit, 0)
    for h in range(heads):
        out_ref[:, head(h)] = (acc_ref[h] / sum_ref[h : h + 1, :]).T.astype(jnp.bfloat16)
    mass_ref[...] = max_ref[...] + jnp.log2(sum_ref[...])


def backward_kernel(
    heads, lens_ref, q_ref, win_ref, att_ref, grad_ref, mass_ref, dq_ref, keep_ref, send_ref, acc_ref, delta_ref
):
    rows = q_ref.shape[0]
    score_scale = 1.0 / math.sqrt(HEAD_WIDTH)
    scale = LOG2_E * score_scale
    place, first, base = window_place(rows)
    positions, starts, start = doc_rows(lens_ref, first, rows)
    acc_ref[...] = jnp.zeros_like(acc_ref)
    keep_ref[...] = jnp.zeros_like(keep_ref)
    send_ref[...] = jnp.zeros_like(send_ref)
    ones = jnp.ones((8, HEAD_WIDTH), jnp.float32)
    for h in range(heads):
        product = grad_ref[:, head(h)].astype(jnp.float32) * att_ref[:, head(h)].astype(jnp.float32)
        sums = lax.dot_general(
            ones, product, NT, preferred_element_type=jnp.float32, precision=lax.Precision.HIGHEST
        )
        delta_ref[h : h + 1, :] = sums[0:1, :]

    def visit(block, carry):
        keys = win_ref[block, 0]
        values = win_ref[block, 1]
        keys_t = keys.T
        bias = block_bias(block, base, rows, positions, starts)
        key_grad = jnp.zeros((rows, HEAD_WIDTH), jnp.float32)
        value_grad = jnp.zeros((rows, HEAD_WIDTH), jnp.float32)
        for h in range(heads):
            q_head = q_ref[:, head(h)]
            grad_head = grad_ref[:, head(h)]
            scores = (
                lax.dot_general(keys, q_head, NT, preferred_element_type=jnp.float32) * scale + bias
            )
            prob = jnp.exp2(scores - mass_ref[h : h + 1, :])
            grad_prob = lax.dot_general(values, grad_head, NT, preferred_element_type=jnp.float32)
            grad_score = (prob * (grad_prob - delta_ref[h : h + 1, :])).astype(jnp.bfloat16)
            value_grad = value_grad + jnp.dot(
                prob.astype(jnp.bfloat16), grad_head, preferred_element_type=jnp.float32
            )
            key_grad = key_grad + jnp.dot(grad_score, q_head, preferred_element_type=jnp.float32)
            acc_ref[h] += jnp.dot(keys_t, grad_score, preferred_element_type=jnp.float32)
        key_grad = key_grad * score_scale
        core, slot = window_slot(block, place)

        @pl.when(core == 0)
        def _():
            keep_ref[slot, 0] = key_grad
            keep_ref[slot, 1] = value_grad

        @pl.when(core == 1)
        def _():
            send_ref[slot, 0] = key_grad.astype(jnp.bfloat16)
            send_ref[slot, 1] = value_grad.astype(jnp.bfloat16)

        return carry

    lax.fori_loop((start - base) // rows, BACK * GROUP + place + 1, visit, 0)
    for h in range(heads):
        dq_ref[:, head(h)] = (acc_ref[h] * score_scale).T.astype(jnp.bfloat16)


def whole(shape=None):
    return pl.BlockSpec(memory_space=pltpu.VMEM)


SCALARS = pl.BlockSpec(memory_space=pltpu.SMEM)


def attend(doc_lengths, queries, parts):
    rows, width = queries.shape
    heads = width // HEAD_WIDTH
    visits = (REACH + 1) * heads * rows * rows
    return pl.pallas_call(
        partial(forward_kernel, heads),
        out_shape=(
            jax.ShapeDtypeStruct((rows, width), jnp.bfloat16),
            jax.ShapeDtypeStruct((heads, rows), jnp.float32),
            jax.ShapeDtypeStruct((WINDOW, 2, rows, HEAD_WIDTH), jnp.bfloat16),
        ),
        in_specs=[SCALARS] + [whole()] * (1 + len(parts)),
        out_specs=(whole(), whole(), whole()),
        scratch_shapes=[
            pltpu.VMEM((heads, HEAD_WIDTH, rows), jnp.float32),
            pltpu.VMEM((heads, rows), jnp.float32),
            pltpu.VMEM((heads, rows), jnp.float32),
        ],
        compiler_params=params(24),
        cost_estimate=pl.CostEstimate(
            flops=4 * visits * HEAD_WIDTH, bytes_accessed=4 * 2**20, transcendentals=visits
        ),
        name="attend",
    )(doc_lengths, queries, *parts)


def attend_back(doc_lengths, queries, window, attention, grad, mass):
    rows, width = queries.shape
    heads = width // HEAD_WIDTH
    visits = (REACH + 1) * heads * rows * rows
    parts_shape = (2 * PLANES, 2, rows, HEAD_WIDTH)
    return pl.pallas_call(
        partial(backward_kernel, heads),
        out_shape=(
            jax.ShapeDtypeStruct((rows, width), jnp.bfloat16),
            jax.ShapeDtypeStruct(parts_shape, jnp.float32),
            jax.ShapeDtypeStruct(parts_shape, jnp.bfloat16),
        ),
        in_specs=[SCALARS] + [whole()] * 5,
        out_specs=(whole(), whole(), whole()),
        scratch_shapes=[
            pltpu.VMEM((heads, HEAD_WIDTH, rows), jnp.float32),
            pltpu.VMEM((heads, rows), jnp.float32),
        ],
        compiler_params=params(32),
        cost_estimate=pl.CostEstimate(
            flops=10 * visits * HEAD_WIDTH, bytes_accessed=8 * 2**20, transcendentals=visits
        ),
        name="attend_back",
    )(doc_lengths, queries, window, attention, grad, mass)


def project_kernel(half_ref, att_ref, weight_ref, *rest):
    out_ref = rest[-1]
    total = jnp.dot(att_ref[...], weight_ref[...], preferred_element_type=jnp.float32).astype(jnp.bfloat16)
    if len(rest) == 2:
        total = (total.astype(jnp.float32) + rest[0][...].astype(jnp.float32)).astype(jnp.bfloat16)
    out_ref[...] = total


def project(half, attention, weight, other=None, tile=512):
    rows, depth = attention.shape
    columns = weight.shape[1] // 2
    steps = columns // tile
    in_specs = [
        pl.BlockSpec((rows, depth), lambda i, half_ref: (0, 0)),
        pl.BlockSpec((depth, tile), lambda i, half_ref: (0, half_ref[0] * steps + i)),
    ]
    operands = [attention, weight]
    if other is not None:
        in_specs.append(pl.BlockSpec((rows, tile), lambda i, half_ref: (0, i)))
        operands.append(other)
    return pl.pallas_call(
        project_kernel,
        out_shape=jax.ShapeDtypeStruct((rows, columns), jnp.bfloat16),
        grid_spec=pltpu.PrefetchScalarGridSpec(
            num_scalar_prefetch=1,
            grid=(steps,),
            in_specs=in_specs,
            out_specs=pl.BlockSpec((rows, tile), lambda i, half_ref: (0, i)),
        ),
        compiler_params=params(16),
        cost_estimate=pl.CostEstimate(
            flops=2 * rows * depth * columns, bytes_accessed=2 * depth * columns, transcendentals=0
        ),
        name="project",
    )(half, *operands)


def grad_kernel(half_ref, cot_ref, weight_ref, *rest):
    out_ref = rest[-1]
    total = lax.dot_general(cot_ref[...], weight_ref[...], NT, preferred_element_type=jnp.float32)
    if len(rest) == 2:
        total = total + rest[0][...]
    out_ref[...] = total.astype(out_ref.dtype)


def project_back(half, cot, weight, before=None, tile=256):
    rows, columns = cot.shape
    depth = weight.shape[0]
    in_specs = [
        pl.BlockSpec((rows, columns), lambda i, half_ref: (0, 0)),
        pl.BlockSpec((tile, columns), lambda i, half_ref: (i, half_ref[0])),
    ]
    operands = [cot, weight]
    if before is not None:
        in_specs.append(pl.BlockSpec((rows, tile), lambda i, half_ref: (0, i)))
        operands.append(before)
    return pl.pallas_call(
        grad_kernel,
        out_shape=jax.ShapeDtypeStruct((rows, depth), jnp.float32 if before is None else jnp.bfloat16),
        grid_spec=pltpu.PrefetchScalarGridSpec(
            num_scalar_prefetch=1,
            grid=(depth // tile,),
            in_specs=in_specs,
            out_specs=pl.BlockSpec((rows, tile), lambda i, half_ref: (0, i)),
        ),
        compiler_params=params(16),
        cost_estimate=pl.CostEstimate(
            flops=2 * rows * depth * columns, bytes_accessed=2 * depth * columns, transcendentals=0
        ),
        name="project_back",
    )(half, *operands)


def body(queries, keys, values, out_weight, cotangent, doc_lengths):
    mine = lax.axis_index("tp").astype(jnp.int32).reshape(1)
    theirs = 1 - mine
    same = [(keys, values)]
    for plane in range(1, PLANES):
        same.append(tuple(shifted(block, plane * GROUP) for block in (keys, values)))
    other_cot = tp_swapped(cotangent)
    other = [tuple(swapped(block, 2) for block in pair) for pair in same]
    near = same + other
    far = [tuple(swapped(block, 1) for block in pair) for pair in near]
    parts = [block for pair in near + far for block in pair]
    own_grad = project_back(mine, cotangent, out_weight)
    attention, mass, window = attend(doc_lengths, queries, parts)
    other_mixed = tp_swapped(project(theirs, attention, out_weight))
    grad = project_back(theirs, other_cot, out_weight, own_grad)
    query_grad, keep, send = attend_back(doc_lengths, queries, window, attention, grad, mass)
    core_sum = keep + swapped(send, 1).astype(jnp.float32)
    half_back = swapped(core_sum[PLANES:].astype(jnp.bfloat16), 2)
    half_sum = core_sum[:PLANES] + half_back.astype(jnp.float32)
    totals = half_sum[0]
    for plane in range(1, PLANES):
        totals = totals + shifted(
            half_sum[plane].astype(jnp.bfloat16), -plane * GROUP
        ).astype(jnp.float32)
    mixed_out = project(mine, attention, out_weight, other_mixed)
    keys_gradient = totals[0].astype(jnp.bfloat16)
    values_gradient = totals[1].astype(jnp.bfloat16)
    return (mixed_out, query_grad, keys_gradient, values_gradient)


def solution(mesh):
    in_specs = (P("ctx", "tp"), P("ctx", "tp"), P("ctx", "tp"), P("tp", None), P("ctx", "tp"), P())
    out_specs = (P("ctx", "tp"), P("ctx", "tp"), P("ctx", "tp"), P("ctx", "tp"))
    return jax.shard_map(body, mesh=mesh, in_specs=in_specs, out_specs=out_specs, check_vma=False)
```

```python
from functools import partial
import math

import jax
import jax.numpy as jnp
from jax import lax
from jax.experimental import pallas as pl
from jax.experimental.pallas import tpu as pltpu
from jax.sharding import PartitionSpec as P

HEAD_WIDTH = 128
REACH = 8
GROUP = 4
BACK = REACH // GROUP
PLANES = BACK + 1
WINDOW = PLANES * GROUP
LOG2_E = math.log2(math.e)
MASKED = -1e30
NT = (((1,), (1,)), ((), ()))


def shifted(block, distance):
    size = lax.axis_size("ctx")
    route = [(i, i + distance) for i in range(size) if 0 <= i + distance < size]
    return lax.ppermute(block, "ctx", route)


def swapped(block, bit):
    return lax.ppermute(block, "ctx", [(i, i ^ bit) for i in range(lax.axis_size("ctx"))])


def tp_swapped(block):
    return lax.ppermute(block, "tp", [(0, 1), (1, 0)])


def params(mebibytes):
    return pltpu.CompilerParams(vmem_limit_bytes=mebibytes * 2**20)


def window_slot(block, place):
    plane = BACK - block // GROUP
    half = (block // 2 + place // 2) % 2
    core = (block + place) % 2
    return core, half * PLANES + plane


def doc_rows(lens_ref, first, rows):
    positions = first + lax.broadcasted_iota(jnp.int32, (1, rows), 1)

    def add_doc(doc, carry):
        end, starts, start = carry
        length = lens_ref[doc]
        end = end + length
        return (
            end,
            starts + jnp.where(positions >= end, length, 0),
            start + jnp.where(first >= end, length, 0),
        )

    zero = jnp.int32(0)
    _, starts, start = lax.fori_loop(
        0, lens_ref.shape[0], add_doc, (zero, jnp.zeros((1, rows), jnp.int32), zero)
    )
    return positions, starts, start


def block_bias(block, base, rows, positions, starts):
    key_pos = base + block * rows + lax.broadcasted_iota(jnp.int32, (rows, rows), 0)
    return jnp.where((key_pos >= starts) & (key_pos <= positions), 0.0, MASKED).astype(jnp.float32)


def head(h):
    return slice(h * HEAD_WIDTH, (h + 1) * HEAD_WIDTH)


def window_place(rows):
    device = lax.axis_index("ctx")
    place = device % GROUP
    first = device * rows
    base = first - (BACK * GROUP + place) * rows
    return place, first, base


def forward_kernel(heads, lens_ref, qt_ref, *rest):
    parts = rest[: 4 * PLANES]
    out_ref, mass_ref, win_ref, acc_ref, max_ref, sum_ref, score_ref, prob_ref = rest[4 * PLANES :]
    rows = qt_ref.shape[2]
    scale = LOG2_E / math.sqrt(HEAD_WIDTH)
    place, first, base = window_place(rows)
    positions, starts, start = doc_rows(lens_ref, first, rows)
    for core in range(2):
        for slot in range(2 * PLANES):
            plane, half = slot % PLANES, slot // PLANES
            where = (BACK - plane) * GROUP + (place ^ (half * 2 + core))
            win_ref[where] = parts[core * 2 * PLANES + slot][...]
    acc_ref[...] = jnp.zeros_like(acc_ref)
    max_ref[...] = jnp.full_like(max_ref, MASKED)
    sum_ref[...] = jnp.zeros_like(sum_ref)

    def visit(block, carry):
        keys = win_ref[block, 0]
        values_t = win_ref[block, 1].T
        bias = block_bias(block, base, rows, positions, starts)
        for h in range(heads):
            score_ref[h] = jnp.dot(keys, qt_ref[h], preferred_element_type=jnp.float32)
        for h in range(heads):
            scores = score_ref[h] * scale + bias
            old_max = max_ref[h : h + 1, :]
            new_max = jnp.maximum(old_max, jnp.max(scores, axis=0, keepdims=True))
            prob = jnp.exp2(scores - new_max)
            alpha = jnp.exp2(old_max - new_max)
            max_ref[h : h + 1, :] = new_max
            sum_ref[h : h + 1, :] = sum_ref[h : h + 1, :] * alpha + jnp.sum(
                prob, axis=0, keepdims=True
            )
            prob_ref[h] = prob.astype(jnp.bfloat16)
            acc_ref[h] = acc_ref[h] * alpha
        for h in range(heads):
            acc_ref[h] += jnp.dot(values_t, prob_ref[h], preferred_element_type=jnp.float32)
        return carry

    lax.fori_loop((start - base) // rows, BACK * GROUP + place + 1, visit, 0)
    for h in range(heads):
        out_ref[:, head(h)] = (acc_ref[h] / sum_ref[h : h + 1, :]).T.astype(jnp.bfloat16)
    mass_ref[...] = max_ref[...] + jnp.log2(sum_ref[...])


def backward_kernel(
    heads,
    lens_ref,
    q_ref,
    qt_ref,
    win_ref,
    att_ref,
    grad_ref,
    grad_t_ref,
    mass_ref,
    dq_ref,
    keep_ref,
    send_ref,
    acc_ref,
    delta_ref,
    wide_mass_ref,
    prob_ref,
    grad_score_ref,
    bias_ref,
):
    rows = q_ref.shape[0]
    score_scale = 1.0 / math.sqrt(HEAD_WIDTH)
    scale = LOG2_E * score_scale
    place, first, base = window_place(rows)
    positions, starts, start = doc_rows(lens_ref, first, rows)
    acc_ref[...] = jnp.zeros_like(acc_ref)
    keep_ref[...] = jnp.zeros_like(keep_ref)
    send_ref[...] = jnp.zeros_like(send_ref)
    mass_t = mass_ref[...].T
    for h in range(heads):
        product = grad_ref[:, head(h)].astype(jnp.float32) * att_ref[:, head(h)].astype(jnp.float32)
        delta_ref[h] = jnp.broadcast_to(
            jnp.sum(product, axis=1, keepdims=True), (rows, HEAD_WIDTH)
        )
        wide_mass_ref[h] = jnp.broadcast_to(mass_t[:, h : h + 1], (rows, HEAD_WIDTH))
    chunk = HEAD_WIDTH

    def across(ref, h, piece):
        return jnp.concatenate([ref[h, piece]] * (rows // HEAD_WIDTH), axis=1)

    def visit(block, carry):
        keys = win_ref[block, 0]
        keys_t = keys.T
        values_t = win_ref[block, 1].T
        bias_ref[...] = block_bias(block, base, rows, positions, starts).T
        for h in range(heads):
            for at in range(0, rows, chunk):
                piece = slice(at, at + chunk)
                scores = (
                    jnp.dot(q_ref[piece, head(h)], keys_t, preferred_element_type=jnp.float32) * scale
                    + bias_ref[piece]
                )
                prob = jnp.exp2(scores - across(wide_mass_ref, h, piece))
                prob_ref[h, piece] = prob.astype(jnp.bfloat16)
                grad_prob = jnp.dot(
                    grad_ref[piece, head(h)], values_t, preferred_element_type=jnp.float32
                )
                grad_score_ref[h, piece] = (
                    prob * (grad_prob - across(delta_ref, h, piece))
                ).astype(jnp.bfloat16)
        key_grad = jnp.zeros((HEAD_WIDTH, rows), jnp.float32)
        value_grad = jnp.zeros((HEAD_WIDTH, rows), jnp.float32)
        for h in range(heads):
            value_grad = value_grad + jnp.dot(
                grad_t_ref[h], prob_ref[h], preferred_element_type=jnp.float32
            )
        for h in range(heads):
            key_grad = key_grad + jnp.dot(
                qt_ref[h], grad_score_ref[h], preferred_element_type=jnp.float32
            )
        for h in range(heads):
            acc_ref[h] += jnp.dot(grad_score_ref[h], keys, preferred_element_type=jnp.float32)
        key_grad = key_grad.T * score_scale
        value_grad = value_grad.T
        core, slot = window_slot(block, place)

        @pl.when(core == 0)
        def _():
            keep_ref[slot, 0] = key_grad
            keep_ref[slot, 1] = value_grad

        @pl.when(core == 1)
        def _():
            send_ref[slot, 0] = key_grad.astype(jnp.bfloat16)
            send_ref[slot, 1] = value_grad.astype(jnp.bfloat16)

        return carry

    lax.fori_loop((start - base) // rows, BACK * GROUP + place + 1, visit, 0)
    for h in range(heads):
        dq_ref[:, head(h)] = (acc_ref[h] * score_scale).astype(jnp.bfloat16)


def whole(shape=None):
    return pl.BlockSpec(memory_space=pltpu.VMEM)


SCALARS = pl.BlockSpec(memory_space=pltpu.SMEM)


def attend(doc_lengths, queries_t, parts):
    heads, _, rows = queries_t.shape
    visits = (REACH + 1) * heads * rows * rows
    return pl.pallas_call(
        partial(forward_kernel, heads),
        out_shape=(
            jax.ShapeDtypeStruct((rows, heads * HEAD_WIDTH), jnp.bfloat16),
            jax.ShapeDtypeStruct((heads, rows), jnp.float32),
            jax.ShapeDtypeStruct((WINDOW, 2, rows, HEAD_WIDTH), jnp.bfloat16),
        ),
        in_specs=[SCALARS] + [whole()] * (1 + len(parts)),
        out_specs=(whole(), whole(), whole()),
        scratch_shapes=[
            pltpu.VMEM((heads, HEAD_WIDTH, rows), jnp.float32),
            pltpu.VMEM((heads, rows), jnp.float32),
            pltpu.VMEM((heads, rows), jnp.float32),
            pltpu.VMEM((heads, rows, rows), jnp.float32),
            pltpu.VMEM((heads, rows, rows), jnp.bfloat16),
        ],
        compiler_params=params(24),
        cost_estimate=pl.CostEstimate(
            flops=4 * visits * HEAD_WIDTH, bytes_accessed=4 * 2**20, transcendentals=visits
        ),
        name="attend",
    )(doc_lengths, queries_t, *parts)


def attend_back(doc_lengths, queries, queries_t, window, attention, grad, grad_t, mass):
    rows, width = queries.shape
    heads = width // HEAD_WIDTH
    visits = (REACH + 1) * heads * rows * rows
    parts_shape = (2 * PLANES, 2, rows, HEAD_WIDTH)
    return pl.pallas_call(
        partial(backward_kernel, heads),
        out_shape=(
            jax.ShapeDtypeStruct((rows, width), jnp.bfloat16),
            jax.ShapeDtypeStruct(parts_shape, jnp.float32),
            jax.ShapeDtypeStruct(parts_shape, jnp.bfloat16),
        ),
        in_specs=[SCALARS] + [whole()] * 7,
        out_specs=(whole(), whole(), whole()),
        scratch_shapes=[
            pltpu.VMEM((heads, rows, HEAD_WIDTH), jnp.float32),
            pltpu.VMEM((heads, rows, HEAD_WIDTH), jnp.float32),
            pltpu.VMEM((heads, rows, HEAD_WIDTH), jnp.float32),
            pltpu.VMEM((heads, rows, rows), jnp.bfloat16),
            pltpu.VMEM((heads, rows, rows), jnp.bfloat16),
            pltpu.VMEM((rows, rows), jnp.float32),
        ],
        compiler_params=params(32),
        cost_estimate=pl.CostEstimate(
            flops=10 * visits * HEAD_WIDTH, bytes_accessed=8 * 2**20, transcendentals=visits
        ),
        name="attend_back",
    )(doc_lengths, queries, queries_t, window, attention, grad, grad_t, mass)


def pair_kernel(keys_ref, values_ref, out_ref):
    out_ref[0] = keys_ref[...]
    out_ref[1] = values_ref[...]


def pair_up(keys, values):
    return pl.pallas_call(
        pair_kernel,
        out_shape=jax.ShapeDtypeStruct((2,) + keys.shape, keys.dtype),
        in_specs=[whole()] * 2,
        out_specs=whole(),
        compiler_params=params(8),
        name="pair_up",
    )(keys, values)


def project_kernel(half_ref, att_ref, weight_ref, *rest):
    out_ref = rest[-1]
    total = jnp.dot(att_ref[...], weight_ref[...], preferred_element_type=jnp.float32).astype(jnp.bfloat16)
    if len(rest) == 2:
        total = (total.astype(jnp.float32) + rest[0][...].astype(jnp.float32)).astype(jnp.bfloat16)
    out_ref[...] = total


def project(half, attention, weight, other=None, tile=512):
    rows, depth = attention.shape
    columns = weight.shape[1] // 2
    steps = columns // tile
    in_specs = [
        pl.BlockSpec((rows, depth), lambda i, half_ref: (0, 0)),
        pl.BlockSpec((depth, tile), lambda i, half_ref: (0, half_ref[0] * steps + i)),
    ]
    operands = [attention, weight]
    if other is not None:
        in_specs.append(pl.BlockSpec((rows, tile), lambda i, half_ref: (0, i)))
        operands.append(other)
    return pl.pallas_call(
        project_kernel,
        out_shape=jax.ShapeDtypeStruct((rows, columns), jnp.bfloat16),
        grid_spec=pltpu.PrefetchScalarGridSpec(
            num_scalar_prefetch=1,
            grid=(steps,),
            in_specs=in_specs,
            out_specs=pl.BlockSpec((rows, tile), lambda i, half_ref: (0, i)),
        ),
        compiler_params=params(16),
        cost_estimate=pl.CostEstimate(
            flops=2 * rows * depth * columns, bytes_accessed=2 * depth * columns, transcendentals=0
        ),
        name="project",
    )(half, *operands)


def transpose_heads(wide_ref, out_ref):
    for h in range(out_ref.shape[0]):
        out_ref[h] = wide_ref[:, head(h)].T


def own_grad_kernel(half_ref, cot_ref, weight_ref, q_ref, out_ref, qt_ref):
    out_ref[...] = lax.dot_general(
        cot_ref[...], weight_ref[...], NT, preferred_element_type=jnp.float32
    )
    transpose_heads(q_ref, qt_ref)


def other_grad_kernel(half_ref, cot_ref, weight_ref, before_ref, out_ref, out_t_ref):
    total = lax.dot_general(
        cot_ref[...], weight_ref[...], NT, preferred_element_type=jnp.float32
    )
    out_ref[...] = (total + before_ref[...]).astype(jnp.bfloat16)
    transpose_heads(out_ref, out_t_ref)


def project_back(kernel, half, cot, weight, tiled, out_type, tile=256):
    rows, columns = cot.shape
    depth = weight.shape[0]
    tile_heads = tile // HEAD_WIDTH
    return pl.pallas_call(
        kernel,
        out_shape=(
            jax.ShapeDtypeStruct((rows, depth), out_type),
            jax.ShapeDtypeStruct((depth // HEAD_WIDTH, HEAD_WIDTH, rows), jnp.bfloat16),
        ),
        grid_spec=pltpu.PrefetchScalarGridSpec(
            num_scalar_prefetch=1,
            grid=(depth // tile,),
            in_specs=[
                pl.BlockSpec((rows, columns), lambda i, half_ref: (0, 0)),
                pl.BlockSpec((tile, columns), lambda i, half_ref: (i, half_ref[0])),
                pl.BlockSpec((rows, tile), lambda i, half_ref: (0, i)),
            ],
            out_specs=(
                pl.BlockSpec((rows, tile), lambda i, half_ref: (0, i)),
                pl.BlockSpec((tile_heads, HEAD_WIDTH, rows), lambda i, half_ref: (i, 0, 0)),
            ),
        ),
        compiler_params=params(16),
        cost_estimate=pl.CostEstimate(
            flops=2 * rows * depth * columns, bytes_accessed=2 * depth * columns, transcendentals=0
        ),
        name="project_back",
    )(half, cot, weight, tiled)


def body(queries, keys, values, out_weight, cotangent, doc_lengths):
    mine = lax.axis_index("tp").astype(jnp.int32).reshape(1)
    theirs = 1 - mine
    other_cot = tp_swapped(cotangent)
    pair = pair_up(keys, values)
    back = [shifted(pair, plane * GROUP) for plane in range(1, PLANES)]
    across = swapped(pair, 2)
    own_grad, queries_t = project_back(
        own_grad_kernel, mine, cotangent, out_weight, queries, jnp.float32
    )
    back, own_grad = lax.optimization_barrier((back, own_grad))
    near = [pair] + back + [across] + [swapped(block, 2) for block in back]
    parts = near + [swapped(block, 1) for block in near]
    attention, mass, window = attend(doc_lengths, queries_t, parts)
    other_term = project(theirs, attention, out_weight)
    other_mixed = tp_swapped(other_term)
    other_cot, other_term = lax.optimization_barrier((other_cot, other_term))
    grad, grad_t = project_back(
        other_grad_kernel, theirs, other_cot, out_weight, own_grad, jnp.bfloat16
    )
    query_grad, keep, send = attend_back(
        doc_lengths, queries, queries_t, window, attention, grad, grad_t, mass
    )
    core_sum = keep + swapped(send, 1).astype(jnp.float32)
    half_back = swapped(core_sum[PLANES:].astype(jnp.bfloat16), 2)
    half_sum = core_sum[:PLANES] + half_back.astype(jnp.float32)
    totals = half_sum[0]
    for plane in range(1, PLANES):
        totals = totals + shifted(
            half_sum[plane].astype(jnp.bfloat16), -plane * GROUP
        ).astype(jnp.float32)
    mixed_out = project(mine, attention, out_weight, other_mixed)
    keys_gradient = totals[0].astype(jnp.bfloat16)
    values_gradient = totals[1].astype(jnp.bfloat16)
    return (mixed_out, query_grad, keys_gradient, values_gradient)


def solution(mesh):
    in_specs = (P("ctx", "tp"), P("ctx", "tp"), P("ctx", "tp"), P("tp", None), P("ctx", "tp"), P())
    out_specs = (P("ctx", "tp"), P("ctx", "tp"), P("ctx", "tp"), P("ctx", "tp"))
    return jax.shard_map(body, mesh=mesh, in_specs=in_specs, out_specs=out_specs, check_vma=False)
```

```python
from functools import partial
import math

import jax
import jax.numpy as jnp
from jax import lax
from jax.experimental import pallas as pl
from jax.experimental.pallas import tpu as pltpu
from jax.sharding import PartitionSpec as P

HEAD_WIDTH = 128
REACH = 8
GROUP = 4
BACK = REACH // GROUP
PLANES = BACK + 1
WINDOW = PLANES * GROUP
LOG2_E = math.log2(math.e)
MASKED = -1e30
NT = (((1,), (1,)), ((), ()))


def shifted(block, distance):
    size = lax.axis_size("ctx")
    route = [(i, i + distance) for i in range(size) if 0 <= i + distance < size]
    return lax.ppermute(block, "ctx", route)


def swapped(block, bit):
    return lax.ppermute(block, "ctx", [(i, i ^ bit) for i in range(lax.axis_size("ctx"))])


def tp_swapped(block):
    return lax.ppermute(block, "tp", [(0, 1), (1, 0)])


def params(mebibytes):
    return pltpu.CompilerParams(vmem_limit_bytes=mebibytes * 2**20)


def window_slot(block, place):
    plane = BACK - block // GROUP
    half = (block // 2 + place // 2) % 2
    core = (block + place) % 2
    return core, half * PLANES + plane


def doc_rows(lens_ref, first, rows):
    positions = first + lax.broadcasted_iota(jnp.int32, (1, rows), 1)

    def add_doc(doc, carry):
        end, starts, start = carry
        length = lens_ref[doc]
        end = end + length
        return (
            end,
            starts + jnp.where(positions >= end, length, 0),
            start + jnp.where(first >= end, length, 0),
        )

    zero = jnp.int32(0)
    _, starts, start = lax.fori_loop(
        0, lens_ref.shape[0], add_doc, (zero, jnp.zeros((1, rows), jnp.int32), zero)
    )
    return positions, starts, start


def block_bias(block, base, rows, positions, starts):
    key_pos = base + block * rows + lax.broadcasted_iota(jnp.int32, (rows, rows), 0)
    return jnp.where((key_pos >= starts) & (key_pos <= positions), 0.0, MASKED).astype(jnp.float32)


def head(h):
    return slice(h * HEAD_WIDTH, (h + 1) * HEAD_WIDTH)


def window_place(rows):
    device = lax.axis_index("ctx")
    place = device % GROUP
    first = device * rows
    base = first - (BACK * GROUP + place) * rows
    return place, first, base


def forward_kernel(heads, planes, last, lens_ref, qt_ref, *rest):
    count = len(planes) * GROUP
    parts, rest = rest[:count], rest[count:]
    if last:
        acc_in, max_in, sum_in, win_in = rest[:4]
        out_ref, mass_ref, win_ref, acc_ref, max_ref, sum_ref, score_ref, prob_ref = rest[4:]
    else:
        acc_ref, max_ref, sum_ref, win_ref, score_ref, prob_ref = rest
    rows = qt_ref.shape[2]
    scale = LOG2_E / math.sqrt(HEAD_WIDTH)
    place, first, base = window_place(rows)
    positions, starts, start = doc_rows(lens_ref, first, rows)
    for at, plane in enumerate(planes):
        for way in range(GROUP):
            where = (BACK - plane) * GROUP + (place ^ way)
            win_ref[where] = parts[at * GROUP + way][...]
    if last:
        acc_ref[...] = acc_in[...]
        max_ref[...] = max_in[...]
        sum_ref[...] = sum_in[...]
        kept = (BACK + 1 - planes[0]) * GROUP
        win_ref[kept:] = win_in[kept:]
    else:
        acc_ref[...] = jnp.zeros_like(acc_ref)
        max_ref[...] = jnp.full_like(max_ref, MASKED)
        sum_ref[...] = jnp.zeros_like(sum_ref)

    def visit(block, carry):
        keys = win_ref[block, 0]
        values_t = win_ref[block, 1].T
        bias = block_bias(block, base, rows, positions, starts)
        for h in range(heads):
            score_ref[h] = jnp.dot(keys, qt_ref[h], preferred_element_type=jnp.float32)
        for h in range(heads):
            scores = score_ref[h] * scale + bias
            old_max = max_ref[h : h + 1, :]
            new_max = jnp.maximum(old_max, jnp.max(scores, axis=0, keepdims=True))
            prob = jnp.exp2(scores - new_max)
            alpha = jnp.exp2(old_max - new_max)
            max_ref[h : h + 1, :] = new_max
            sum_ref[h : h + 1, :] = sum_ref[h : h + 1, :] * alpha + jnp.sum(
                prob, axis=0, keepdims=True
            )
            prob_ref[h] = prob.astype(jnp.bfloat16)
            acc_ref[h] = acc_ref[h] * alpha
        for h in range(heads):
            acc_ref[h] += jnp.dot(values_t, prob_ref[h], preferred_element_type=jnp.float32)
        return carry

    lowest = (BACK - planes[-1]) * GROUP
    highest = (BACK - planes[0] + 1) * GROUP
    lax.fori_loop(
        jnp.maximum((start - base) // rows, lowest),
        jnp.minimum(BACK * GROUP + place + 1, highest),
        visit,
        0,
    )
    if last:
        for h in range(heads):
            out_ref[:, head(h)] = (acc_ref[h] / sum_ref[h : h + 1, :]).T.astype(jnp.bfloat16)
        mass_ref[...] = max_ref[...] + jnp.log2(sum_ref[...])


def backward_kernel(
    heads,
    lens_ref,
    q_ref,
    qt_ref,
    win_ref,
    att_ref,
    grad_ref,
    grad_t_ref,
    mass_ref,
    dq_ref,
    keep_ref,
    send_ref,
    acc_ref,
    delta_ref,
    wide_mass_ref,
    prob_ref,
    grad_score_ref,
    bias_ref,
):
    rows = q_ref.shape[0]
    score_scale = 1.0 / math.sqrt(HEAD_WIDTH)
    scale = LOG2_E * score_scale
    place, first, base = window_place(rows)
    positions, starts, start = doc_rows(lens_ref, first, rows)
    acc_ref[...] = jnp.zeros_like(acc_ref)
    keep_ref[...] = jnp.zeros_like(keep_ref)
    send_ref[...] = jnp.zeros_like(send_ref)
    mass_t = mass_ref[...].T
    for h in range(heads):
        product = grad_ref[:, head(h)].astype(jnp.float32) * att_ref[:, head(h)].astype(jnp.float32)
        delta_ref[h] = jnp.broadcast_to(
            jnp.sum(product, axis=1, keepdims=True), (rows, HEAD_WIDTH)
        )
        wide_mass_ref[h] = jnp.broadcast_to(mass_t[:, h : h + 1], (rows, HEAD_WIDTH))
    chunk = HEAD_WIDTH

    def across(ref, h, piece):
        return jnp.concatenate([ref[h, piece]] * (rows // HEAD_WIDTH), axis=1)

    def visit(block, carry):
        keys = win_ref[block, 0]
        keys_t = keys.T
        values_t = win_ref[block, 1].T
        bias_ref[...] = block_bias(block, base, rows, positions, starts).T
        for h in range(heads):
            for at in range(0, rows, chunk):
                piece = slice(at, at + chunk)
                scores = (
                    jnp.dot(q_ref[piece, head(h)], keys_t, preferred_element_type=jnp.float32) * scale
                    + bias_ref[piece]
                )
                prob = jnp.exp2(scores - across(wide_mass_ref, h, piece))
                prob_ref[h, piece] = prob.astype(jnp.bfloat16)
                grad_prob = jnp.dot(
                    grad_ref[piece, head(h)], values_t, preferred_element_type=jnp.float32
                )
                grad_score_ref[h, piece] = (
                    prob * (grad_prob - across(delta_ref, h, piece))
                ).astype(jnp.bfloat16)
        key_grad = jnp.zeros((HEAD_WIDTH, rows), jnp.float32)
        value_grad = jnp.zeros((HEAD_WIDTH, rows), jnp.float32)
        for h in range(heads):
            value_grad = value_grad + jnp.dot(
                grad_t_ref[h], prob_ref[h], preferred_element_type=jnp.float32
            )
        for h in range(heads):
            key_grad = key_grad + jnp.dot(
                qt_ref[h], grad_score_ref[h], preferred_element_type=jnp.float32
            )
        for h in range(heads):
            acc_ref[h] += jnp.dot(grad_score_ref[h], keys, preferred_element_type=jnp.float32)
        key_grad = key_grad.T * score_scale
        value_grad = value_grad.T
        core, slot = window_slot(block, place)

        @pl.when(core == 0)
        def _():
            keep_ref[slot, 0] = key_grad
            keep_ref[slot, 1] = value_grad

        @pl.when(core == 1)
        def _():
            send_ref[slot, 0] = key_grad.astype(jnp.bfloat16)
            send_ref[slot, 1] = value_grad.astype(jnp.bfloat16)

        return carry

    lax.fori_loop((start - base) // rows, BACK * GROUP + place + 1, visit, 0)
    for h in range(heads):
        dq_ref[:, head(h)] = (acc_ref[h] * score_scale).astype(jnp.bfloat16)


def whole(shape=None):
    return pl.BlockSpec(memory_space=pltpu.VMEM)


SCALARS = pl.BlockSpec(memory_space=pltpu.SMEM)


def attend(doc_lengths, queries_t, planes, parts, before=()):
    heads, _, rows = queries_t.shape
    last = len(before) > 0
    visits = len(planes) * GROUP * heads * rows * rows
    sums = [(heads, HEAD_WIDTH, rows), (heads, rows), (heads, rows)]
    window = jax.ShapeDtypeStruct((WINDOW, 2, rows, HEAD_WIDTH), jnp.bfloat16)
    working = [
        pltpu.VMEM((heads, rows, rows), jnp.float32),
        pltpu.VMEM((heads, rows, rows), jnp.bfloat16),
    ]
    if last:
        out_shape = (
            jax.ShapeDtypeStruct((rows, heads * HEAD_WIDTH), jnp.bfloat16),
            jax.ShapeDtypeStruct((heads, rows), jnp.float32),
            window,
        )
        working = [pltpu.VMEM(shape, jnp.float32) for shape in sums] + working
    else:
        out_shape = tuple(jax.ShapeDtypeStruct(shape, jnp.float32) for shape in sums) + (window,)
    return pl.pallas_call(
        partial(forward_kernel, heads, planes, last),
        out_shape=out_shape,
        in_specs=[SCALARS] + [whole()] * (1 + len(parts) + len(before)),
        out_specs=(whole(),) * len(out_shape),
        scratch_shapes=working,
        compiler_params=params(12),
        cost_estimate=pl.CostEstimate(
            flops=4 * visits * HEAD_WIDTH, bytes_accessed=4 * 2**20, transcendentals=visits
        ),
        name="attend",
    )(doc_lengths, queries_t, *parts, *before)


def turn_kernel(wide_ref, out_ref):
    transpose_heads(wide_ref, out_ref)


def turned(wide):
    rows, width = wide.shape
    return pl.pallas_call(
        turn_kernel,
        out_shape=jax.ShapeDtypeStruct((width // HEAD_WIDTH, HEAD_WIDTH, rows), wide.dtype),
        in_specs=[whole()],
        out_specs=whole(),
        compiler_params=params(4),
        name="turned",
    )(wide)


def attend_back(doc_lengths, queries, queries_t, window, attention, grad, grad_t, mass):
    rows, width = queries.shape
    heads = width // HEAD_WIDTH
    visits = (REACH + 1) * heads * rows * rows
    parts_shape = (2 * PLANES, 2, rows, HEAD_WIDTH)
    return pl.pallas_call(
        partial(backward_kernel, heads),
        out_shape=(
            jax.ShapeDtypeStruct((rows, width), jnp.bfloat16),
            jax.ShapeDtypeStruct(parts_shape, jnp.float32),
            jax.ShapeDtypeStruct(parts_shape, jnp.bfloat16),
        ),
        in_specs=[SCALARS] + [whole()] * 7,
        out_specs=(whole(), whole(), whole()),
        scratch_shapes=[
            pltpu.VMEM((heads, rows, HEAD_WIDTH), jnp.float32),
            pltpu.VMEM((heads, rows, HEAD_WIDTH), jnp.float32),
            pltpu.VMEM((heads, rows, HEAD_WIDTH), jnp.float32),
            pltpu.VMEM((heads, rows, rows), jnp.bfloat16),
            pltpu.VMEM((heads, rows, rows), jnp.bfloat16),
            pltpu.VMEM((rows, rows), jnp.float32),
        ],
        compiler_params=params(16),
        cost_estimate=pl.CostEstimate(
            flops=10 * visits * HEAD_WIDTH, bytes_accessed=8 * 2**20, transcendentals=visits
        ),
        name="attend_back",
    )(doc_lengths, queries, queries_t, window, attention, grad, grad_t, mass)


def pair_kernel(keys_ref, values_ref, out_ref, sems):
    copies = [
        pltpu.make_async_copy(ref, out_ref.at[kind], sems.at[kind])
        for kind, ref in enumerate((keys_ref, values_ref))
    ]
    for copy in copies:
        copy.start()
    for copy in copies:
        copy.wait()


def pair_up(keys, values):
    return pl.pallas_call(
        pair_kernel,
        out_shape=jax.ShapeDtypeStruct((2,) + keys.shape, keys.dtype),
        in_specs=[pl.BlockSpec(memory_space=pl.ANY)] * 2,
        out_specs=whole(),
        scratch_shapes=[pltpu.SemaphoreType.DMA((2,))],
        compiler_params=params(4),
        name="pair_up",
    )(keys, values)


def project_kernel(tile, pieces, half_ref, att_ref, weight_ref, *rest):
    others, outs = rest[: len(rest) - pieces], rest[len(rest) - pieces :]
    columns = weight_ref.shape[1] // 2
    first = half_ref[0] * columns
    part = columns // max(len(others), pieces)
    for at in range(0, columns, tile):
        piece = pl.ds(pl.multiple_of(first + at, tile), tile)
        total = jnp.dot(
            att_ref[...], weight_ref[:, piece], preferred_element_type=jnp.float32
        ).astype(jnp.bfloat16)
        if others:
            other = others[at // part][:, at % part : at % part + tile].astype(jnp.float32)
            total = (total.astype(jnp.float32) + other).astype(jnp.bfloat16)
            outs[0][:, at : at + tile] = total
        else:
            outs[at // part][:, at % part : at % part + tile] = total


def project(half, attention, weight, *other, pieces=1, tile=512):
    rows, depth = attention.shape
    columns = weight.shape[1] // 2
    piece = jax.ShapeDtypeStruct((rows, columns // pieces), jnp.bfloat16)
    return pl.pallas_call(
        partial(project_kernel, tile, pieces),
        out_shape=(piece,) * pieces,
        in_specs=[SCALARS] + [whole()] * (2 + len(other)),
        out_specs=(whole(),) * pieces,
        compiler_params=params(8),
        cost_estimate=pl.CostEstimate(
            flops=2 * rows * depth * columns, bytes_accessed=2 * depth * columns, transcendentals=0
        ),
        name="project",
    )(half, attention, weight, *other)


def transpose_heads(wide_ref, out_ref):
    for h in range(out_ref.shape[0]):
        out_ref[h] = wide_ref[:, head(h)].T


def grad_kernel(tile, order_ref, *refs):
    halves, (weight_ref, out_ref, out_t_ref) = refs[:2], refs[2:]
    columns = halves[0].shape[1]
    for at in range(0, weight_ref.shape[0], tile):
        total = 0.0
        for side, cot_ref in enumerate(halves):
            piece = pl.ds(pl.multiple_of(order_ref[side] * columns, columns), columns)
            total += lax.dot_general(
                cot_ref[...], weight_ref[at : at + tile, piece], NT, preferred_element_type=jnp.float32
            )
        out_ref[:, at : at + tile] = total.astype(jnp.bfloat16)
    transpose_heads(out_ref, out_t_ref)


def attention_grad(order, halves, weight, tile=256):
    rows, columns = halves[0].shape
    depth = weight.shape[0]
    return pl.pallas_call(
        partial(grad_kernel, tile),
        out_shape=(
            jax.ShapeDtypeStruct((rows, depth), jnp.bfloat16),
            jax.ShapeDtypeStruct((depth // HEAD_WIDTH, HEAD_WIDTH, rows), jnp.bfloat16),
        ),
        in_specs=[SCALARS] + [whole()] * 3,
        out_specs=(whole(), whole()),
        compiler_params=params(8),
        cost_estimate=pl.CostEstimate(
            flops=4 * rows * depth * columns, bytes_accessed=4 * depth * columns, transcendentals=0
        ),
        name="attention_grad",
    )(order, *halves, weight)


def body(queries, keys, values, out_weight, cotangent, doc_lengths):
    mine = lax.axis_index("tp").astype(jnp.int32).reshape(1)
    theirs = 1 - mine
    order = jnp.concatenate([mine, theirs])
    pair = pair_up(keys, values)
    other_cot = tp_swapped(cotangent)
    planes = [pair] + [shifted(pair, plane * GROUP) for plane in range(1, PLANES)]
    queries_t = turned(queries)

    def group_of(block):
        pairs = [block, swapped(block, 2)]
        return [pairs[0], swapped(pairs[0], 1), pairs[1], swapped(pairs[1], 1)]

    groups = [group_of(block) for block in planes]
    early = tuple(range(BACK))
    sums = attend(doc_lengths, queries_t, early, sum((groups[plane] for plane in early), []))
    attention, mass, window = attend(doc_lengths, queries_t, (BACK,), groups[BACK], sums)
    other_terms = project(theirs, attention, out_weight, pieces=2)
    early_mixed = tp_swapped(other_terms[0])
    other_cot, other_terms = lax.optimization_barrier((other_cot, other_terms))
    grad, grad_t = attention_grad(order, (cotangent, other_cot), out_weight)
    query_grad, keep, send = attend_back(
        doc_lengths, queries, queries_t, window, attention, grad, grad_t, mass
    )
    send, early_mixed = lax.optimization_barrier((send, early_mixed))
    late_mixed = tp_swapped(other_terms[1])
    received = swapped(send, 1)

    def core_sum(slot):
        return keep[slot] + received[slot].astype(jnp.float32)

    crossed = [
        swapped(core_sum(PLANES + plane).astype(jnp.bfloat16), 2) for plane in reversed(range(PLANES))
    ][::-1]
    half_sum = [core_sum(plane) + crossed[plane].astype(jnp.float32) for plane in range(PLANES)]
    totals = half_sum[0]
    for plane in reversed(range(1, PLANES)):
        totals = totals + shifted(
            half_sum[plane].astype(jnp.bfloat16), -plane * GROUP
        ).astype(jnp.float32)
    (mixed_out,) = project(mine, attention, out_weight, early_mixed, late_mixed)
    keys_gradient = totals[0].astype(jnp.bfloat16)
    values_gradient = totals[1].astype(jnp.bfloat16)
    return (mixed_out, query_grad, keys_gradient, values_gradient)


def solution(mesh):
    in_specs = (P("ctx", "tp"), P("ctx", "tp"), P("ctx", "tp"), P("tp", None), P("ctx", "tp"), P())
    out_specs = (P("ctx", "tp"), P("ctx", "tp"), P("ctx", "tp"), P("ctx", "tp"))
    return jax.shard_map(body, mesh=mesh, in_specs=in_specs, out_specs=out_specs, check_vma=False)
```

```python
from functools import partial
import math

import jax
import jax.numpy as jnp
from jax import lax
from jax.experimental import pallas as pl
from jax.experimental.pallas import tpu as pltpu
from jax.sharding import PartitionSpec as P

HEAD_WIDTH = 128
REACH = 8
GROUP = 4
BACK = REACH // GROUP
PLANES = BACK + 1
WINDOW = PLANES * GROUP
LOG2_E = math.log2(math.e)
MASKED = -1e30
EXCESS = 64.0
SUM_ROWS = 16
NT = (((1,), (1,)), ((), ()))


def shifted(block, distance):
    size = lax.axis_size("ctx")
    route = [(i, i + distance) for i in range(size) if 0 <= i + distance < size]
    return lax.ppermute(block, "ctx", route)


def swapped(block, bit):
    return lax.ppermute(block, "ctx", [(i, i ^ bit) for i in range(lax.axis_size("ctx"))])


def tp_swapped(block):
    return lax.ppermute(block, "tp", [(0, 1), (1, 0)])


def params(mebibytes):
    return pltpu.CompilerParams(vmem_limit_bytes=mebibytes * 2**20)


def window_slot(block, place):
    plane = BACK - block // GROUP
    half = (block // 2 + place // 2) % 2
    core = (block + place) % 2
    return core, half * PLANES + plane


def doc_rows(lens_ref, first, rows):
    positions = first + lax.broadcasted_iota(jnp.int32, (1, rows), 1)

    def add_doc(doc, carry):
        end, starts, start = carry
        length = lens_ref[doc]
        end = end + length
        return (
            end,
            starts + jnp.where(positions >= end, length, 0),
            start + jnp.where(first >= end, length, 0),
        )

    zero = jnp.int32(0)
    _, starts, start = lax.fori_loop(
        0, lens_ref.shape[0], add_doc, (zero, jnp.zeros((1, rows), jnp.int32), zero)
    )
    return starts, start


def block_bias(block, base, first, starts):
    rows = starts.shape[1]
    key_pos = base + block * rows + lax.broadcasted_iota(jnp.int32, (rows, rows), 0)
    positions = first + lax.broadcasted_iota(jnp.int32, (1, rows), 1)
    return jnp.where((key_pos >= starts) & (key_pos <= positions), 0.0, MASKED).astype(jnp.float32)


def head(h):
    return slice(h * HEAD_WIDTH, (h + 1) * HEAD_WIDTH)


def window_place(rows):
    device = lax.axis_index("ctx")
    place = device % GROUP
    first = device * rows
    base = first - (BACK * GROUP + place) * rows
    return place, first, base


def forward_kernel(heads, planes, last, begin_ref, starts_ref, qt_ref, *rest):
    count = len(planes) * GROUP
    parts, rest = rest[:count], rest[count:]
    if last:
        acc_in, shift_in, win_in = rest[:3]
        out_ref, mass_ref, win_ref, acc_ref, shift_ref, score_ref, prob_ref, most_ref = rest[3:]
    else:
        acc_ref, shift_ref, win_ref, score_ref, prob_ref, most_ref = rest
    rows = qt_ref.shape[2]
    scale = LOG2_E / math.sqrt(HEAD_WIDTH)
    place, first, base = window_place(rows)
    begin = begin_ref[0]
    own = BACK * GROUP + place
    starts = starts_ref[0:1, :]
    in_first = starts <= jnp.min(starts, axis=1, keepdims=True)
    for at, plane in enumerate(planes):
        for way in range(GROUP):
            where = (BACK - plane) * GROUP + (place ^ way)
            win_ref[where] = parts[at * GROUP + way][...]
    if last:
        kept = (BACK + 1 - planes[0]) * GROUP
        win_ref[kept:] = win_in[kept:]

    def values_of(block):
        ones = jnp.ones((SUM_ROWS, rows), jnp.bfloat16)
        return jnp.concatenate([values_turned(win_ref, block), ones], axis=0)

    def weigh(values_t, h):
        return jnp.dot(values_t, prob_ref[h], preferred_element_type=jnp.float32)

    def visit_own():
        keys, values_t = win_ref[own, 0], values_of(own)
        bias = block_bias(own, base, first, starts)
        for h in range(heads):
            score_ref[h] = jnp.dot(keys, qt_ref[h], preferred_element_type=jnp.float32)
        for h in range(heads):
            scores = score_ref[h] * scale + bias
            shift = jnp.max(scores, axis=0, keepdims=True)
            shift_ref[h : h + 1, :] = shift
            prob_ref[h] = jnp.exp2(scores - shift).astype(jnp.bfloat16)
        for h in range(heads):
            acc_ref[h] = weigh(values_t, h)

    def visit(block, masked):
        keys, values_t = win_ref[block, 0], values_of(block)
        if masked:
            bias = block_bias(block, base, first, starts)
        for h in range(heads):
            shift = jnp.where(in_first, shift_ref[h : h + 1, :], -MASKED)
            scores = jnp.dot(keys, qt_ref[h], preferred_element_type=jnp.float32) * scale - shift
            if masked:
                scores = scores + bias
            most_ref[h : h + 1, :] = jnp.maximum(
                most_ref[h : h + 1, :], jnp.max(scores, axis=0, keepdims=True)
            )
            prob_ref[h] = jnp.exp2(scores).astype(jnp.bfloat16)
        for h in range(heads):
            acc_ref[h] += weigh(values_t, h)

    def visit_following(block):
        keys, values_t = win_ref[block, 0], values_of(block)
        bias = block_bias(block, base, first, starts)
        for h in range(heads):
            score_ref[h] = jnp.dot(keys, qt_ref[h], preferred_element_type=jnp.float32)
        for h in range(heads):
            scores = score_ref[h] * scale + bias
            old_shift = shift_ref[h : h + 1, :]
            shift = jnp.maximum(old_shift, jnp.max(scores, axis=0, keepdims=True))
            shift_ref[h : h + 1, :] = shift
            prob_ref[h] = jnp.exp2(scores - shift).astype(jnp.bfloat16)
            acc_ref[h] = acc_ref[h] * jnp.exp2(old_shift - shift)
        for h in range(heads):
            acc_ref[h] += weigh(values_t, h)

    lowest = (BACK - planes[-1]) * GROUP
    end = jnp.minimum(own, (BACK - planes[0] + 1) * GROUP)

    def begin_sums():
        if last:
            acc_ref[...] = acc_in[...]
            shift_ref[...] = shift_in[...]
        else:
            visit_own()

    begin_sums()
    most_ref[...] = jnp.full_like(most_ref, MASKED)

    @pl.when((begin >= lowest) & (begin < end))
    def _():
        visit(begin, True)

    pl.loop(jnp.maximum(begin + 1, lowest), end)(lambda block: visit(block, False))

    @pl.when(jnp.max(most_ref[...]) > EXCESS)
    def _():
        begin_sums()
        pl.loop(jnp.maximum(begin, lowest), end)(visit_following)

    if last:
        for h in range(heads):
            total = acc_ref[h, HEAD_WIDTH : HEAD_WIDTH + 1, :]
            mass_ref[h : h + 1, :] = shift_ref[h : h + 1, :] + jnp.log2(total)
            out_ref[:, head(h)] = (acc_ref[h, :HEAD_WIDTH] / total).T.astype(jnp.bfloat16)


def backward_kernel(
    heads,
    begin_ref,
    starts_ref,
    q_ref,
    qt_ref,
    win_ref,
    att_ref,
    grad_ref,
    grad_t_ref,
    mass_ref,
    dq_ref,
    keep_ref,
    send_ref,
    acc_ref,
    delta_ref,
    wide_mass_ref,
    prob_ref,
    grad_score_ref,
    bias_ref,
):
    rows = q_ref.shape[0]
    score_scale = 1.0 / math.sqrt(HEAD_WIDTH)
    scale = LOG2_E * score_scale
    place, first, base = window_place(rows)
    starts = starts_ref[0:1, :]
    mass_t = mass_ref[...].T
    for h in range(heads):
        product = grad_ref[:, head(h)].astype(jnp.float32) * att_ref[:, head(h)].astype(jnp.float32)
        delta_ref[h] = jnp.broadcast_to(
            jnp.sum(product, axis=1, keepdims=True), (rows, HEAD_WIDTH)
        )
        wide_mass_ref[h] = jnp.broadcast_to(mass_t[:, h : h + 1], (rows, HEAD_WIDTH))
    chunk = HEAD_WIDTH
    own = BACK * GROUP + place

    def across(ref, h, piece):
        return jnp.concatenate([ref[h, piece]] * (rows // HEAD_WIDTH), axis=1)

    def visit(block, own_block):
        keys = win_ref[block, 0]
        keys_t = keys.T
        values_t = values_turned(win_ref, block)
        bias_ref[...] = block_bias(block, base, first, starts).T
        for h in range(heads):
            for at in range(0, rows, chunk):
                piece = slice(at, at + chunk)
                scores = (
                    jnp.dot(q_ref[piece, head(h)], keys_t, preferred_element_type=jnp.float32) * scale
                    + bias_ref[piece]
                )
                prob = jnp.exp2(scores - across(wide_mass_ref, h, piece))
                prob_ref[h, piece] = prob.astype(jnp.bfloat16)
                grad_prob = jnp.dot(
                    grad_ref[piece, head(h)], values_t, preferred_element_type=jnp.float32
                )
                grad_score_ref[h, piece] = (
                    prob * (grad_prob - across(delta_ref, h, piece))
                ).astype(jnp.bfloat16)
        key_grad = jnp.zeros((HEAD_WIDTH, rows), jnp.float32)
        value_grad = jnp.zeros((HEAD_WIDTH, rows), jnp.float32)
        for h in range(heads):
            value_grad = value_grad + jnp.dot(
                grad_t_ref[h], prob_ref[h], preferred_element_type=jnp.float32
            )
        for h in range(heads):
            key_grad = key_grad + jnp.dot(
                qt_ref[h], grad_score_ref[h], preferred_element_type=jnp.float32
            )
        for h in range(heads):
            query_grad = jnp.dot(grad_score_ref[h], keys, preferred_element_type=jnp.float32)
            if own_block:
                acc_ref[h] = query_grad
            else:
                acc_ref[h] += query_grad
        give(block, key_grad * score_scale, value_grad)

    def give(block, key_grad, value_grad):
        core, slot = window_slot(block, place)

        @pl.when(core == 0)
        def _():
            keep_ref[slot, 0] = key_grad
            keep_ref[slot, 1] = value_grad

        @pl.when(core == 1)
        def _():
            send_ref[slot, 0] = key_grad.astype(jnp.bfloat16)
            send_ref[slot, 1] = value_grad.astype(jnp.bfloat16)

    def give_nothing(block):
        none = jnp.zeros((HEAD_WIDTH, rows), jnp.float32)
        give(block, none, none)

    visit(own, True)
    pl.loop(begin_ref[0], own)(lambda block: visit(block, False))
    pl.loop(0, begin_ref[0])(give_nothing)
    pl.loop(own + 1, WINDOW)(give_nothing)
    for h in range(heads):
        dq_ref[:, head(h)] = (acc_ref[h] * score_scale).astype(jnp.bfloat16)


def whole(shape=None):
    return pl.BlockSpec(memory_space=pltpu.VMEM)


SCALARS = pl.BlockSpec(memory_space=pltpu.SMEM)


def attend(prepared, planes, parts, before=()):
    queries_t, starts, begin = prepared
    heads, _, rows = queries_t.shape
    last = len(before) > 0
    visits = len(planes) * GROUP * heads * rows * rows
    sums = [(heads, HEAD_WIDTH + SUM_ROWS, rows), (heads, rows)]
    window = jax.ShapeDtypeStruct((WINDOW, 2, rows, HEAD_WIDTH), jnp.bfloat16)
    working = [
        pltpu.VMEM((heads, rows, rows), jnp.float32),
        pltpu.VMEM((heads, rows, rows), jnp.bfloat16),
        pltpu.VMEM((heads, rows), jnp.float32),
    ]
    if last:
        out_shape = (
            jax.ShapeDtypeStruct((rows, heads * HEAD_WIDTH), jnp.bfloat16),
            jax.ShapeDtypeStruct((heads, rows), jnp.float32),
            window,
        )
        working = [pltpu.VMEM(shape, jnp.float32) for shape in sums] + working
    else:
        out_shape = tuple(jax.ShapeDtypeStruct(shape, jnp.float32) for shape in sums) + (window,)
    return pl.pallas_call(
        partial(forward_kernel, heads, planes, last),
        out_shape=out_shape,
        in_specs=[SCALARS] + [whole()] * (2 + len(parts) + len(before)),
        out_specs=(whole(),) * len(out_shape),
        scratch_shapes=working,
        compiler_params=params(12),
        cost_estimate=pl.CostEstimate(
            flops=4 * visits * HEAD_WIDTH, bytes_accessed=4 * 2**20, transcendentals=visits
        ),
        name="attend",
    )(begin, starts, queries_t, *parts, *before)


def prepare_kernel(lens_ref, wide_ref, out_ref, starts_ref, begin_ref):
    rows = wide_ref.shape[0]
    _, first, base = window_place(rows)
    starts, start = doc_rows(lens_ref, first, rows)
    starts_ref[...] = jnp.broadcast_to(starts, starts_ref.shape)
    begin_ref[0] = (start - base) // rows
    transpose_heads(wide_ref, out_ref)


def prepare(doc_lengths, queries):
    rows, width = queries.shape
    return pl.pallas_call(
        prepare_kernel,
        out_shape=(
            jax.ShapeDtypeStruct((width // HEAD_WIDTH, HEAD_WIDTH, rows), queries.dtype),
            jax.ShapeDtypeStruct((8, rows), jnp.int32),
            jax.ShapeDtypeStruct((1,), jnp.int32),
        ),
        in_specs=[SCALARS, whole()],
        out_specs=(whole(), whole(), SCALARS),
        compiler_params=params(4),
        name="prepare",
    )(doc_lengths, queries)


def attend_back(prepared, queries, window, attention, grad, grad_t, mass):
    queries_t, starts, begin = prepared
    rows, width = queries.shape
    heads = width // HEAD_WIDTH
    visits = (REACH + 1) * heads * rows * rows
    parts_shape = (2 * PLANES, 2, HEAD_WIDTH, rows)
    return pl.pallas_call(
        partial(backward_kernel, heads),
        out_shape=(
            jax.ShapeDtypeStruct((rows, width), jnp.bfloat16),
            jax.ShapeDtypeStruct(parts_shape, jnp.float32),
            jax.ShapeDtypeStruct(parts_shape, jnp.bfloat16),
        ),
        in_specs=[SCALARS] + [whole()] * 8,
        out_specs=(whole(), whole(), whole()),
        scratch_shapes=[
            pltpu.VMEM((heads, rows, HEAD_WIDTH), jnp.float32),
            pltpu.VMEM((heads, rows, HEAD_WIDTH), jnp.float32),
            pltpu.VMEM((heads, rows, HEAD_WIDTH), jnp.float32),
            pltpu.VMEM((heads, rows, rows), jnp.bfloat16),
            pltpu.VMEM((heads, rows, rows), jnp.bfloat16),
            pltpu.VMEM((rows, rows), jnp.float32),
        ],
        compiler_params=params(16),
        cost_estimate=pl.CostEstimate(
            flops=10 * visits * HEAD_WIDTH, bytes_accessed=8 * 2**20, transcendentals=visits
        ),
        name="attend_back",
    )(begin, starts, queries, queries_t, window, attention, grad, grad_t, mass)


def pair_kernel(keys_ref, values_ref, out_ref):
    out_ref[0] = keys_ref[...]
    turned = values_ref[...].T
    for at in range(0, turned.shape[1], HEAD_WIDTH):
        out_ref[1, at : at + HEAD_WIDTH] = turned[:, at : at + HEAD_WIDTH]


def pair_up(keys, values):
    return pl.pallas_call(
        pair_kernel,
        out_shape=jax.ShapeDtypeStruct((2,) + keys.shape, keys.dtype),
        in_specs=[whole()] * 2,
        out_specs=whole(),
        compiler_params=params(4),
        name="pair_up",
    )(keys, values)


def values_turned(win_ref, block):
    rows = win_ref.shape[2]
    return jnp.concatenate(
        [win_ref[block, 1, at : at + HEAD_WIDTH] for at in range(0, rows, HEAD_WIDTH)], axis=1
    )


def finish_kernel(keep_ref, received_ref, *rest):
    others, outs = rest[:-2], rest[-2:]
    for kind, out_ref in enumerate(outs):
        total = keep_ref[0, kind] + received_ref[0, kind].astype(jnp.float32)
        for other in others:
            total = total + other[kind].astype(jnp.float32)
        out_ref[...] = total.T.astype(jnp.bfloat16)


def finish(keep, received, others):
    _, _, width, rows = keep.shape
    out = jax.ShapeDtypeStruct((rows, width), jnp.bfloat16)
    return pl.pallas_call(
        finish_kernel,
        out_shape=(out, out),
        in_specs=[whole()] * (2 + len(others)),
        out_specs=(whole(), whole()),
        compiler_params=params(4),
        name="finish",
    )(keep, received, *others)


def project_kernel(tile, pieces, half_ref, att_ref, weight_ref, *rest):
    others, outs = rest[: len(rest) - pieces], rest[len(rest) - pieces :]
    columns = weight_ref.shape[1] // 2
    at = 0
    for part in others or outs:
        for there in range(0, part.shape[1], tile):
            piece = pl.ds(pl.multiple_of(half_ref[0] * columns + at, tile), tile)
            total = jnp.dot(
                att_ref[...], weight_ref[:, piece], preferred_element_type=jnp.float32
            ).astype(jnp.bfloat16)
            if others:
                other = part[:, there : there + tile].astype(jnp.float32)
                total = (total.astype(jnp.float32) + other).astype(jnp.bfloat16)
                outs[0][:, at : at + tile] = total
            else:
                part[:, there : there + tile] = total
            at += tile


def project(half, attention, weight, *other, eighths=(8,)):
    rows, depth = attention.shape
    columns = weight.shape[1] // 2
    tile = columns // 8
    pieces = len(eighths)
    shapes = [(rows, columns * part // 8) for part in eighths]
    return pl.pallas_call(
        partial(project_kernel, tile, pieces),
        out_shape=tuple(jax.ShapeDtypeStruct(shape, jnp.bfloat16) for shape in shapes),
        in_specs=[SCALARS] + [whole()] * (2 + len(other)),
        out_specs=(whole(),) * pieces,
        compiler_params=params(8),
        cost_estimate=pl.CostEstimate(
            flops=2 * rows * depth * columns, bytes_accessed=2 * depth * columns, transcendentals=0
        ),
        name="project",
    )(half, attention, weight, *other)


def transpose_heads(wide_ref, out_ref):
    for h in range(out_ref.shape[0]):
        out_ref[h] = wide_ref[:, head(h)].T


def grad_kernel(tile, order_ref, *refs):
    halves, (weight_ref, out_ref, out_t_ref) = refs[:2], refs[2:]
    columns = halves[0].shape[1]
    for at in range(0, weight_ref.shape[0], tile):
        total = 0.0
        for side, cot_ref in enumerate(halves):
            piece = pl.ds(pl.multiple_of(order_ref[side] * columns, columns), columns)
            total += lax.dot_general(
                cot_ref[...], weight_ref[at : at + tile, piece], NT, preferred_element_type=jnp.float32
            )
        out_ref[:, at : at + tile] = total.astype(jnp.bfloat16)
    transpose_heads(out_ref, out_t_ref)


def attention_grad(order, halves, weight, tile=256):
    rows, columns = halves[0].shape
    depth = weight.shape[0]
    return pl.pallas_call(
        partial(grad_kernel, tile),
        out_shape=(
            jax.ShapeDtypeStruct((rows, depth), jnp.bfloat16),
            jax.ShapeDtypeStruct((depth // HEAD_WIDTH, HEAD_WIDTH, rows), jnp.bfloat16),
        ),
        in_specs=[SCALARS] + [whole()] * 3,
        out_specs=(whole(), whole()),
        compiler_params=params(8),
        cost_estimate=pl.CostEstimate(
            flops=4 * rows * depth * columns, bytes_accessed=4 * depth * columns, transcendentals=0
        ),
        name="attention_grad",
    )(order, *halves, weight)


def body(queries, keys, values, out_weight, cotangent, doc_lengths):
    mine = lax.axis_index("tp").astype(jnp.int32).reshape(1)
    theirs = 1 - mine
    order = jnp.concatenate([mine, theirs])
    pair = pair_up(keys, values)
    other_cot = tp_swapped(cotangent)
    planes = [pair] + [shifted(pair, plane * GROUP) for plane in range(1, PLANES)]
    prepared = prepare(doc_lengths, queries)
    planes[BACK], *prepared = lax.optimization_barrier((planes[BACK], *prepared))

    def group_of(block):
        half = swapped(block, 2)
        return [block, swapped(block, 1), half, swapped(half, 1)]

    def last_group_of(block):
        pairs = [block, swapped(block, 1)]
        return pairs + [swapped(each, 2) for each in pairs]

    groups = [group_of(block) for block in planes[:BACK]] + [last_group_of(planes[BACK])]
    early = tuple(range(BACK))
    sums = attend(prepared, early, sum((groups[plane] for plane in early), []))
    attention, mass, window = attend(prepared, (BACK,), groups[BACK], sums)
    other_terms = project(theirs, attention, out_weight, eighths=(5, 3))
    early_mixed = tp_swapped(other_terms[0])
    other_cot, other_terms = lax.optimization_barrier((other_cot, other_terms))
    grad, grad_t = attention_grad(order, (cotangent, other_cot), out_weight)
    query_grad, keep, send = attend_back(
        prepared, queries, window, attention, grad, grad_t, mass
    )
    send, early_mixed = lax.optimization_barrier((send, early_mixed))
    late_mixed = tp_swapped(other_terms[1])
    received = swapped(send, 1)

    def core_sum(slots):
        return keep[slots] + received[slots].astype(jnp.float32)

    crossed = {}
    for plane in reversed(range(PLANES)):
        crossed[plane] = swapped(core_sum(PLANES + plane).astype(jnp.bfloat16), 2)
    arrived = []
    for plane in range(1, PLANES):
        half_sum = core_sum(plane) + crossed[plane].astype(jnp.float32)
        arrived.append(shifted(half_sum.astype(jnp.bfloat16), -plane * GROUP))
    (mixed_out,) = project(mine, attention, out_weight, early_mixed, late_mixed)
    keys_gradient, values_gradient = finish(keep, received, [crossed[0]] + arrived)
    return (mixed_out, query_grad, keys_gradient, values_gradient)


def solution(mesh):
    in_specs = (P("ctx", "tp"), P("ctx", "tp"), P("ctx", "tp"), P("tp", None), P("ctx", "tp"), P())
    out_specs = (P("ctx", "tp"), P("ctx", "tp"), P("ctx", "tp"), P("ctx", "tp"))
    return jax.shard_map(body, mesh=mesh, in_specs=in_specs, out_specs=out_specs, check_vma=False)
```

```python
from functools import partial
import math

import jax
import jax.numpy as jnp
from jax import lax
from jax.experimental import pallas as pl
from jax.experimental.pallas import tpu as pltpu
from jax.sharding import PartitionSpec as P

HEAD_WIDTH = 128
REACH = 8
GROUP = 4
BACK = REACH // GROUP
PLANES = BACK + 1
WINDOW = PLANES * GROUP
LOG2_E = math.log2(math.e)
MASKED = -1e30
EXCESS = 64.0
SUM_ROWS = 16
NT = (((1,), (1,)), ((), ()))


def sent_on(block, distance):
    size = lax.axis_size("ctx")
    return lax.ppermute(block, "ctx", [(i, i + distance) for i in range(size - distance)])


def sent_back(block, distance):
    size = lax.axis_size("ctx")
    return lax.ppermute(block, "ctx", [(i, (i - distance) % size) for i in range(size)])


def swapped(block, bit):
    return lax.ppermute(block, "ctx", [(i, i ^ bit) for i in range(lax.axis_size("ctx"))])


def tp_swapped(block):
    return lax.ppermute(block, "tp", [(0, 1), (1, 0)])


def params(mebibytes):
    return pltpu.CompilerParams(vmem_limit_bytes=mebibytes * 2**20)


def window_slot(block, place):
    plane = BACK - block // GROUP
    half = (block // 2 + place // 2) % 2
    core = (block + place) % 2
    return core, half * PLANES + plane


def doc_rows(lens_ref, first, rows):
    positions = first + lax.broadcasted_iota(jnp.int32, (1, rows), 1)

    def add_doc(doc, carry):
        end, starts, start = carry
        length = lens_ref[doc]
        end = end + length
        return (
            end,
            starts + jnp.where(positions >= end, length, 0),
            start + jnp.where(first >= end, length, 0),
        )

    zero = jnp.int32(0)
    _, starts, start = lax.fori_loop(
        0, lens_ref.shape[0], add_doc, (zero, jnp.zeros((1, rows), jnp.int32), zero)
    )
    return starts, start


def block_bias(block, base, first, starts):
    rows = starts.shape[1]
    key_pos = base + block * rows + lax.broadcasted_iota(jnp.int32, (rows, rows), 0)
    positions = first + lax.broadcasted_iota(jnp.int32, (1, rows), 1)
    return jnp.where((key_pos >= starts) & (key_pos <= positions), 0.0, MASKED).astype(jnp.float32)


def head(h):
    return slice(h * HEAD_WIDTH, (h + 1) * HEAD_WIDTH)


def window_place(rows):
    device = lax.axis_index("ctx")
    place = device % GROUP
    first = device * rows
    base = first - (BACK * GROUP + place) * rows
    return place, first, base


def forward_kernel(heads, planes, last, begin_ref, starts_ref, qt_ref, *rest):
    count = len(planes) * GROUP
    parts, rest = rest[:count], rest[count:]
    if last:
        acc_in, shift_in, win_in = rest[:3]
        out_ref, mass_ref, win_ref, acc_ref, shift_ref, score_ref, prob_ref, most_ref = rest[3:]
    else:
        acc_ref, shift_ref, win_ref, score_ref, prob_ref, most_ref = rest
    rows = qt_ref.shape[2]
    scale = LOG2_E / math.sqrt(HEAD_WIDTH)
    place, first, base = window_place(rows)
    begin = begin_ref[0]
    own = BACK * GROUP + place
    starts = starts_ref[0:1, :]
    in_first = starts <= jnp.min(starts, axis=1, keepdims=True)
    for at, plane in enumerate(planes):
        for way in range(GROUP):
            where = (BACK - plane) * GROUP + (place ^ way)
            win_ref[where] = parts[at * GROUP + way][...]
    if last:
        kept = (BACK + 1 - planes[0]) * GROUP
        win_ref[kept:] = win_in[kept:]

    def values_of(block):
        ones = jnp.ones((SUM_ROWS, rows), jnp.bfloat16)
        return jnp.concatenate([values_turned(win_ref, block), ones], axis=0)

    def weigh(values_t, h):
        return jnp.dot(values_t, prob_ref[h], preferred_element_type=jnp.float32)

    def visit_own():
        keys, values_t = win_ref[own, 0], values_of(own)
        bias = block_bias(own, base, first, starts)
        for h in range(heads):
            score_ref[h] = jnp.dot(keys, qt_ref[h], preferred_element_type=jnp.float32)
        for h in range(heads):
            scores = score_ref[h] * scale + bias
            shift = jnp.max(scores, axis=0, keepdims=True)
            shift_ref[h : h + 1, :] = shift
            prob_ref[h] = jnp.exp2(scores - shift).astype(jnp.bfloat16)
        for h in range(heads):
            acc_ref[h] = weigh(values_t, h)

    def visit(block, masked):
        keys, values_t = win_ref[block, 0], values_of(block)
        if masked:
            bias = block_bias(block, base, first, starts)
        for h in range(heads):
            shift = jnp.where(in_first, shift_ref[h : h + 1, :], -MASKED)
            scores = jnp.dot(keys, qt_ref[h], preferred_element_type=jnp.float32) * scale - shift
            if masked:
                scores = scores + bias
            most_ref[h : h + 1, :] = jnp.maximum(
                most_ref[h : h + 1, :], jnp.max(scores, axis=0, keepdims=True)
            )
            prob_ref[h] = jnp.exp2(scores).astype(jnp.bfloat16)
        for h in range(heads):
            acc_ref[h] += weigh(values_t, h)

    def visit_following(block):
        keys, values_t = win_ref[block, 0], values_of(block)
        bias = block_bias(block, base, first, starts)
        for h in range(heads):
            score_ref[h] = jnp.dot(keys, qt_ref[h], preferred_element_type=jnp.float32)
        for h in range(heads):
            scores = score_ref[h] * scale + bias
            old_shift = shift_ref[h : h + 1, :]
            shift = jnp.maximum(old_shift, jnp.max(scores, axis=0, keepdims=True))
            shift_ref[h : h + 1, :] = shift
            prob_ref[h] = jnp.exp2(scores - shift).astype(jnp.bfloat16)
            acc_ref[h] = acc_ref[h] * jnp.exp2(old_shift - shift)
        for h in range(heads):
            acc_ref[h] += weigh(values_t, h)

    lowest = (BACK - planes[-1]) * GROUP
    end = jnp.minimum(own, (BACK - planes[0] + 1) * GROUP)

    def begin_sums():
        if last:
            acc_ref[...] = acc_in[...]
            shift_ref[...] = shift_in[...]
        else:
            visit_own()

    begin_sums()
    most_ref[...] = jnp.full_like(most_ref, MASKED)

    @pl.when((begin >= lowest) & (begin < end))
    def _():
        visit(begin, True)

    pl.loop(jnp.maximum(begin + 1, lowest), end)(lambda block: visit(block, False))

    @pl.when(jnp.max(most_ref[...]) > EXCESS)
    def _():
        begin_sums()
        pl.loop(jnp.maximum(begin, lowest), end)(visit_following)

    if last:
        for h in range(heads):
            total = acc_ref[h, HEAD_WIDTH : HEAD_WIDTH + 1, :]
            mass_ref[h : h + 1, :] = shift_ref[h : h + 1, :] + jnp.log2(total)
            out_ref[:, head(h)] = (acc_ref[h, :HEAD_WIDTH] / total).T.astype(jnp.bfloat16)


def backward_kernel(
    heads,
    begin_ref,
    starts_ref,
    q_ref,
    qt_ref,
    win_ref,
    att_ref,
    grad_ref,
    grad_t_ref,
    mass_ref,
    dq_ref,
    keep_ref,
    send_ref,
    acc_ref,
    delta_ref,
    wide_mass_ref,
    prob_ref,
    grad_score_ref,
    bias_ref,
):
    rows = q_ref.shape[0]
    score_scale = 1.0 / math.sqrt(HEAD_WIDTH)
    scale = LOG2_E * score_scale
    place, first, base = window_place(rows)
    starts = starts_ref[0:1, :]
    mass_t = mass_ref[...].T
    for h in range(heads):
        product = grad_ref[:, head(h)].astype(jnp.float32) * att_ref[:, head(h)].astype(jnp.float32)
        delta_ref[h] = jnp.broadcast_to(
            jnp.sum(product, axis=1, keepdims=True), (rows, HEAD_WIDTH)
        )
        wide_mass_ref[h] = jnp.broadcast_to(mass_t[:, h : h + 1], (rows, HEAD_WIDTH))
    chunk = HEAD_WIDTH
    own = BACK * GROUP + place

    def across(ref, h, piece):
        return jnp.concatenate([ref[h, piece]] * (rows // HEAD_WIDTH), axis=1)

    def visit(block, own_block):
        keys = win_ref[block, 0]
        keys_t = keys.T
        values_t = values_turned(win_ref, block)
        bias_ref[...] = block_bias(block, base, first, starts).T
        for h in range(heads):
            for at in range(0, rows, chunk):
                piece = slice(at, at + chunk)
                scores = (
                    jnp.dot(q_ref[piece, head(h)], keys_t, preferred_element_type=jnp.float32) * scale
                    + bias_ref[piece]
                )
                prob = jnp.exp2(scores - across(wide_mass_ref, h, piece))
                prob_ref[h, piece] = prob.astype(jnp.bfloat16)
                grad_prob = jnp.dot(
                    grad_ref[piece, head(h)], values_t, preferred_element_type=jnp.float32
                )
                grad_score_ref[h, piece] = (
                    prob * (grad_prob - across(delta_ref, h, piece))
                ).astype(jnp.bfloat16)
        key_grad = jnp.zeros((HEAD_WIDTH, rows), jnp.float32)
        value_grad = jnp.zeros((HEAD_WIDTH, rows), jnp.float32)
        for h in range(heads):
            value_grad = value_grad + jnp.dot(
                grad_t_ref[h], prob_ref[h], preferred_element_type=jnp.float32
            )
        for h in range(heads):
            key_grad = key_grad + jnp.dot(
                qt_ref[h], grad_score_ref[h], preferred_element_type=jnp.float32
            )
        for h in range(heads):
            query_grad = jnp.dot(grad_score_ref[h], keys, preferred_element_type=jnp.float32)
            if own_block:
                acc_ref[h] = query_grad
            else:
                acc_ref[h] += query_grad
        give(block, key_grad * score_scale, value_grad)

    def give(block, key_grad, value_grad):
        core, slot = window_slot(block, place)

        @pl.when(core == 0)
        def _():
            keep_ref[slot, 0] = key_grad
            keep_ref[slot, 1] = value_grad

        @pl.when(core == 1)
        def _():
            send_ref[slot, 0] = key_grad.astype(jnp.bfloat16)
            send_ref[slot, 1] = value_grad.astype(jnp.bfloat16)

    def give_nothing(block):
        none = jnp.zeros((HEAD_WIDTH, rows), jnp.float32)
        give(block, none, none)

    visit(own, True)
    pl.loop(begin_ref[0], own)(lambda block: visit(block, False))
    pl.loop(0, begin_ref[0])(give_nothing)
    pl.loop(own + 1, WINDOW)(give_nothing)
    for h in range(heads):
        dq_ref[:, head(h)] = (acc_ref[h] * score_scale).astype(jnp.bfloat16)


def whole(shape=None):
    return pl.BlockSpec(memory_space=pltpu.VMEM)


SCALARS = pl.BlockSpec(memory_space=pltpu.SMEM)


def attend(prepared, planes, parts, before=()):
    queries_t, starts, begin = prepared
    heads, _, rows = queries_t.shape
    last = len(before) > 0
    visits = len(planes) * GROUP * heads * rows * rows
    sums = [(heads, HEAD_WIDTH + SUM_ROWS, rows), (heads, rows)]
    window = jax.ShapeDtypeStruct((WINDOW, 2, rows, HEAD_WIDTH), jnp.bfloat16)
    working = [
        pltpu.VMEM((heads, rows, rows), jnp.float32),
        pltpu.VMEM((heads, rows, rows), jnp.bfloat16),
        pltpu.VMEM((heads, rows), jnp.float32),
    ]
    if last:
        out_shape = (
            jax.ShapeDtypeStruct((rows, heads * HEAD_WIDTH), jnp.bfloat16),
            jax.ShapeDtypeStruct((heads, rows), jnp.float32),
            window,
        )
        working = [pltpu.VMEM(shape, jnp.float32) for shape in sums] + working
    else:
        out_shape = tuple(jax.ShapeDtypeStruct(shape, jnp.float32) for shape in sums) + (window,)
    return pl.pallas_call(
        partial(forward_kernel, heads, planes, last),
        out_shape=out_shape,
        in_specs=[SCALARS] + [whole()] * (2 + len(parts) + len(before)),
        out_specs=(whole(),) * len(out_shape),
        scratch_shapes=working,
        compiler_params=params(12),
        cost_estimate=pl.CostEstimate(
            flops=4 * visits * HEAD_WIDTH, bytes_accessed=4 * 2**20, transcendentals=visits
        ),
        name="attend",
    )(begin, starts, queries_t, *parts, *before)


def prepare_kernel(lens_ref, wide_ref, out_ref, starts_ref, begin_ref):
    rows = wide_ref.shape[0]
    _, first, base = window_place(rows)
    starts, start = doc_rows(lens_ref, first, rows)
    starts_ref[...] = jnp.broadcast_to(starts, starts_ref.shape)
    begin_ref[0] = (start - base) // rows
    transpose_heads(wide_ref, out_ref)


def prepare(doc_lengths, queries):
    rows, width = queries.shape
    return pl.pallas_call(
        prepare_kernel,
        out_shape=(
            jax.ShapeDtypeStruct((width // HEAD_WIDTH, HEAD_WIDTH, rows), queries.dtype),
            jax.ShapeDtypeStruct((8, rows), jnp.int32),
            jax.ShapeDtypeStruct((1,), jnp.int32),
        ),
        in_specs=[SCALARS, whole()],
        out_specs=(whole(), whole(), SCALARS),
        compiler_params=params(4),
        name="prepare",
    )(doc_lengths, queries)


def attend_back(prepared, queries, window, attention, grad, grad_t, mass):
    queries_t, starts, begin = prepared
    rows, width = queries.shape
    heads = width // HEAD_WIDTH
    visits = (REACH + 1) * heads * rows * rows
    parts_shape = (2 * PLANES, 2, HEAD_WIDTH, rows)
    return pl.pallas_call(
        partial(backward_kernel, heads),
        out_shape=(
            jax.ShapeDtypeStruct((rows, width), jnp.bfloat16),
            jax.ShapeDtypeStruct(parts_shape, jnp.float32),
            jax.ShapeDtypeStruct(parts_shape, jnp.bfloat16),
        ),
        in_specs=[SCALARS] + [whole()] * 8,
        out_specs=(whole(), whole(), whole()),
        scratch_shapes=[
            pltpu.VMEM((heads, rows, HEAD_WIDTH), jnp.float32),
            pltpu.VMEM((heads, rows, HEAD_WIDTH), jnp.float32),
            pltpu.VMEM((heads, rows, HEAD_WIDTH), jnp.float32),
            pltpu.VMEM((heads, rows, rows), jnp.bfloat16),
            pltpu.VMEM((heads, rows, rows), jnp.bfloat16),
            pltpu.VMEM((rows, rows), jnp.float32),
        ],
        compiler_params=params(16),
        cost_estimate=pl.CostEstimate(
            flops=10 * visits * HEAD_WIDTH, bytes_accessed=8 * 2**20, transcendentals=visits
        ),
        name="attend_back",
    )(begin, starts, queries, queries_t, window, attention, grad, grad_t, mass)


def pair_kernel(keys_ref, values_ref, out_ref):
    out_ref[0] = keys_ref[...]
    turned = values_ref[...].T
    for at in range(0, turned.shape[1], HEAD_WIDTH):
        out_ref[1, at : at + HEAD_WIDTH] = turned[:, at : at + HEAD_WIDTH]


def pair_up(keys, values):
    return pl.pallas_call(
        pair_kernel,
        out_shape=jax.ShapeDtypeStruct((2,) + keys.shape, keys.dtype),
        in_specs=[whole()] * 2,
        out_specs=whole(),
        compiler_params=params(4),
        name="pair_up",
    )(keys, values)


def values_turned(win_ref, block):
    rows = win_ref.shape[2]
    return jnp.concatenate(
        [win_ref[block, 1, at : at + HEAD_WIDTH] for at in range(0, rows, HEAD_WIDTH)], axis=1
    )


def finish_kernel(keep_ref, received_ref, *rest):
    others, outs = rest[:-2], rest[-2:]
    for kind, out_ref in enumerate(outs):
        total = keep_ref[0, kind] + received_ref[0, kind].astype(jnp.float32)
        for other in others:
            total = total + other[kind].astype(jnp.float32)
        out_ref[...] = total.T.astype(jnp.bfloat16)


def finish(keep, received, others):
    _, _, width, rows = keep.shape
    out = jax.ShapeDtypeStruct((rows, width), jnp.bfloat16)
    return pl.pallas_call(
        finish_kernel,
        out_shape=(out, out),
        in_specs=[whole()] * (2 + len(others)),
        out_specs=(whole(), whole()),
        compiler_params=params(4),
        name="finish",
    )(keep, received, *others)


def project_kernel(tile, pieces, half_ref, att_ref, weight_ref, *rest):
    others, outs = rest[: len(rest) - pieces], rest[len(rest) - pieces :]
    columns = weight_ref.shape[1] // 2
    at = 0
    for part in others or outs:
        for there in range(0, part.shape[1], tile):
            piece = pl.ds(pl.multiple_of(half_ref[0] * columns + at, tile), tile)
            total = jnp.dot(
                att_ref[...], weight_ref[:, piece], preferred_element_type=jnp.float32
            ).astype(jnp.bfloat16)
            if others:
                other = part[:, there : there + tile].astype(jnp.float32)
                total = (total.astype(jnp.float32) + other).astype(jnp.bfloat16)
                outs[0][:, at : at + tile] = total
            else:
                part[:, there : there + tile] = total
            at += tile


def project(half, attention, weight, *other, eighths=(8,)):
    rows, depth = attention.shape
    columns = weight.shape[1] // 2
    tile = columns // 8
    pieces = len(eighths)
    shapes = [(rows, columns * part // 8) for part in eighths]
    return pl.pallas_call(
        partial(project_kernel, tile, pieces),
        out_shape=tuple(jax.ShapeDtypeStruct(shape, jnp.bfloat16) for shape in shapes),
        in_specs=[SCALARS] + [whole()] * (2 + len(other)),
        out_specs=(whole(),) * pieces,
        compiler_params=params(8),
        cost_estimate=pl.CostEstimate(
            flops=2 * rows * depth * columns, bytes_accessed=2 * depth * columns, transcendentals=0
        ),
        name="project",
    )(half, attention, weight, *other)


def transpose_heads(wide_ref, out_ref):
    for h in range(out_ref.shape[0]):
        out_ref[h] = wide_ref[:, head(h)].T


def grad_kernel(tile, order_ref, *refs):
    halves, (weight_ref, out_ref, out_t_ref) = refs[:2], refs[2:]
    columns = halves[0].shape[1]
    for at in range(0, weight_ref.shape[0], tile):
        total = 0.0
        for side, cot_ref in enumerate(halves):
            piece = pl.ds(pl.multiple_of(order_ref[side] * columns, columns), columns)
            total += lax.dot_general(
                cot_ref[...], weight_ref[at : at + tile, piece], NT, preferred_element_type=jnp.float32
            )
        out_ref[:, at : at + tile] = total.astype(jnp.bfloat16)
    transpose_heads(out_ref, out_t_ref)


def attention_grad(order, halves, weight, tile=256):
    rows, columns = halves[0].shape
    depth = weight.shape[0]
    return pl.pallas_call(
        partial(grad_kernel, tile),
        out_shape=(
            jax.ShapeDtypeStruct((rows, depth), jnp.bfloat16),
            jax.ShapeDtypeStruct((depth // HEAD_WIDTH, HEAD_WIDTH, rows), jnp.bfloat16),
        ),
        in_specs=[SCALARS] + [whole()] * 3,
        out_specs=(whole(), whole()),
        compiler_params=params(8),
        cost_estimate=pl.CostEstimate(
            flops=4 * rows * depth * columns, bytes_accessed=4 * depth * columns, transcendentals=0
        ),
        name="attention_grad",
    )(order, *halves, weight)


def body(queries, keys, values, out_weight, cotangent, doc_lengths):
    mine = lax.axis_index("tp").astype(jnp.int32).reshape(1)
    theirs = 1 - mine
    order = jnp.concatenate([mine, theirs])
    pair = pair_up(keys, values)
    other_cot = tp_swapped(cotangent)
    planes = [pair] + [sent_on(pair, plane * GROUP) for plane in range(1, PLANES)]
    prepared = prepare(doc_lengths, queries)
    planes[BACK], *prepared = lax.optimization_barrier((planes[BACK], *prepared))

    def group_of(block):
        half = swapped(block, 2)
        return [block, swapped(block, 1), half, swapped(half, 1)]

    def last_group_of(block):
        pairs = [block, swapped(block, 1)]
        return pairs + [swapped(each, 2) for each in pairs]

    groups = [group_of(block) for block in planes[:BACK]] + [last_group_of(planes[BACK])]
    early = tuple(range(BACK))
    sums = attend(prepared, early, sum((groups[plane] for plane in early), []))
    attention, mass, window = attend(prepared, (BACK,), groups[BACK], sums)
    other_terms = project(theirs, attention, out_weight, eighths=(5, 3))
    early_mixed = tp_swapped(other_terms[0])
    other_cot, other_terms = lax.optimization_barrier((other_cot, other_terms))
    grad, grad_t = attention_grad(order, (cotangent, other_cot), out_weight)
    query_grad, keep, send = attend_back(
        prepared, queries, window, attention, grad, grad_t, mass
    )
    send, early_mixed = lax.optimization_barrier((send, early_mixed))
    late_mixed = tp_swapped(other_terms[1])
    received = swapped(send, 1)

    def core_sum(slots):
        return keep[slots] + received[slots].astype(jnp.float32)

    crossed = {}
    for plane in reversed(range(PLANES)):
        crossed[plane] = swapped(core_sum(PLANES + plane).astype(jnp.bfloat16), 2)
    arrived = []
    for plane in range(1, PLANES):
        half_sum = core_sum(plane) + crossed[plane].astype(jnp.float32)
        arrived.append(sent_back(half_sum.astype(jnp.bfloat16), plane * GROUP))
    (mixed_out,) = project(mine, attention, out_weight, early_mixed, late_mixed)
    keys_gradient, values_gradient = finish(keep, received, [crossed[0]] + arrived)
    return (mixed_out, query_grad, keys_gradient, values_gradient)


def solution(mesh):
    in_specs = (P("ctx", "tp"), P("ctx", "tp"), P("ctx", "tp"), P("tp", None), P("ctx", "tp"), P())
    out_specs = (P("ctx", "tp"), P("ctx", "tp"), P("ctx", "tp"), P("ctx", "tp"))
    return jax.shard_map(body, mesh=mesh, in_specs=in_specs, out_specs=out_specs, check_vma=False)
```

```python
from functools import partial
import math

import jax
import jax.numpy as jnp
from jax import lax
from jax.experimental import pallas as pl
from jax.experimental.pallas import tpu as pltpu
from jax.sharding import PartitionSpec as P

HEAD_WIDTH = 128
REACH = 8
GROUP = 4
BACK = REACH // GROUP
PLANES = BACK + 1
WINDOW = PLANES * GROUP
LOG2_E = math.log2(math.e)
MASKED = -1e30
EXCESS = 64.0
SUM_ROWS = 16
NT = (((1,), (1,)), ((), ()))


def sent_on(block, distance):
    size = lax.axis_size("ctx")
    return lax.ppermute(block, "ctx", [(i, i + distance) for i in range(size - distance)])


def sent_back(block, distance):
    size = lax.axis_size("ctx")
    return lax.ppermute(block, "ctx", [(i, (i - distance) % size) for i in range(size)])


def swapped(block, bit):
    return lax.ppermute(block, "ctx", [(i, i ^ bit) for i in range(lax.axis_size("ctx"))])


def tp_swapped(block):
    return lax.ppermute(block, "tp", [(0, 1), (1, 0)])


def params(mebibytes):
    return pltpu.CompilerParams(vmem_limit_bytes=mebibytes * 2**20)


def window_slot(block, place):
    plane = BACK - block // GROUP
    half = (block // 2 + place // 2) % 2
    core = (block + place) % 2
    return core, half * PLANES + plane


def doc_rows(lens_ref, first, rows):
    positions = first + lax.broadcasted_iota(jnp.int32, (1, rows), 1)

    def add_doc(doc, carry):
        end, starts, start, middle = carry
        length = lens_ref[doc]
        end = end + length
        return (
            end,
            starts + jnp.where(positions >= end, length, 0),
            start + jnp.where(first >= end, length, 0),
            middle + jnp.where(first + rows // 2 >= end, length, 0),
        )

    zero = jnp.int32(0)
    _, starts, start, middle = lax.fori_loop(
        0, lens_ref.shape[0], add_doc, (zero, jnp.zeros((1, rows), jnp.int32), zero, zero)
    )
    return starts, start, middle


def block_bias(block, base, first, starts):
    rows = starts.shape[1]
    key_pos = base + block * rows + lax.broadcasted_iota(jnp.int32, (rows, rows), 0)
    positions = first + lax.broadcasted_iota(jnp.int32, (1, rows), 1)
    return jnp.where((key_pos >= starts) & (key_pos <= positions), 0.0, MASKED).astype(jnp.float32)


def head(h):
    return slice(h * HEAD_WIDTH, (h + 1) * HEAD_WIDTH)


def window_place(rows):
    device = lax.axis_index("ctx")
    place = device % GROUP
    first = device * rows
    base = first - (BACK * GROUP + place) * rows
    return place, first, base


def forward_kernel(heads, planes, last, begin_ref, starts_ref, qt_ref, *rest):
    count = len(planes) * GROUP
    parts, rest = rest[:count], rest[count:]
    if last:
        acc_in, shift_in, win_in = rest[:3]
        out_ref, mass_ref, win_ref, acc_ref, shift_ref, score_ref, prob_ref, most_ref = rest[3:]
    else:
        acc_ref, shift_ref, win_ref, score_ref, prob_ref, most_ref = rest
    rows = qt_ref.shape[2]
    scale = LOG2_E / math.sqrt(HEAD_WIDTH)
    place, first, base = window_place(rows)
    begin = begin_ref[0]
    own = BACK * GROUP + place
    starts = starts_ref[0:1, :]
    in_first = starts <= jnp.min(starts, axis=1, keepdims=True)
    for at, plane in enumerate(planes):
        for way in range(GROUP):
            where = (BACK - plane) * GROUP + (place ^ way)
            win_ref[where] = parts[at * GROUP + way][...]
    if last:
        kept = (BACK + 1 - planes[0]) * GROUP
        win_ref[kept:] = win_in[kept:]

    def values_of(block):
        ones = jnp.ones((SUM_ROWS, rows), jnp.bfloat16)
        return jnp.concatenate([values_turned(win_ref, block), ones], axis=0)

    def weigh(values_t, h):
        return jnp.dot(values_t, prob_ref[h], preferred_element_type=jnp.float32)

    def visit_own():
        keys, values_t = win_ref[own, 0], values_of(own)
        bias = block_bias(own, base, first, starts)
        for h in range(heads):
            score_ref[h] = jnp.dot(keys, qt_ref[h], preferred_element_type=jnp.float32)
        for h in range(heads):
            scores = score_ref[h] * scale + bias
            shift = jnp.max(scores, axis=0, keepdims=True)
            shift_ref[h : h + 1, :] = shift
            prob_ref[h] = jnp.exp2(scores - shift).astype(jnp.bfloat16)
        for h in range(heads):
            acc_ref[h] = weigh(values_t, h)

    def visit(block, masked):
        keys, values_t = win_ref[block, 0], values_of(block)
        if masked:
            bias = block_bias(block, base, first, starts)
        for h in range(heads):
            shift = jnp.where(in_first, shift_ref[h : h + 1, :], -MASKED)
            scores = jnp.dot(keys, qt_ref[h], preferred_element_type=jnp.float32) * scale - shift
            if masked:
                scores = scores + bias
            most_ref[h : h + 1, :] = jnp.maximum(
                most_ref[h : h + 1, :], jnp.max(scores, axis=0, keepdims=True)
            )
            prob_ref[h] = jnp.exp2(scores).astype(jnp.bfloat16)
        for h in range(heads):
            acc_ref[h] += weigh(values_t, h)

    def visit_following(block):
        keys, values_t = win_ref[block, 0], values_of(block)
        bias = block_bias(block, base, first, starts)
        for h in range(heads):
            score_ref[h] = jnp.dot(keys, qt_ref[h], preferred_element_type=jnp.float32)
        for h in range(heads):
            scores = score_ref[h] * scale + bias
            old_shift = shift_ref[h : h + 1, :]
            shift = jnp.maximum(old_shift, jnp.max(scores, axis=0, keepdims=True))
            shift_ref[h : h + 1, :] = shift
            prob_ref[h] = jnp.exp2(scores - shift).astype(jnp.bfloat16)
            acc_ref[h] = acc_ref[h] * jnp.exp2(old_shift - shift)
        for h in range(heads):
            acc_ref[h] += weigh(values_t, h)

    lowest = (BACK - planes[-1]) * GROUP
    end = jnp.minimum(own, (BACK - planes[0] + 1) * GROUP)

    def begin_sums():
        if last:
            acc_ref[...] = acc_in[...]
            shift_ref[...] = shift_in[...]
        else:
            visit_own()

    begin_sums()
    most_ref[...] = jnp.full_like(most_ref, MASKED)

    @pl.when((begin >= lowest) & (begin < end))
    def _():
        visit(begin, True)

    pl.loop(jnp.maximum(begin + 1, lowest), end)(lambda block: visit(block, False))

    @pl.when(jnp.max(most_ref[...]) > EXCESS)
    def _():
        begin_sums()
        pl.loop(jnp.maximum(begin, lowest), end)(visit_following)

    if last:
        for h in range(heads):
            total = acc_ref[h, HEAD_WIDTH : HEAD_WIDTH + 1, :]
            mass_ref[h : h + 1, :] = shift_ref[h : h + 1, :] + jnp.log2(total)
            out_ref[:, head(h)] = (acc_ref[h, :HEAD_WIDTH] / total).T.astype(jnp.bfloat16)


def backward_kernel(
    heads,
    begin_ref,
    starts_ref,
    q_ref,
    qt_ref,
    win_ref,
    att_ref,
    grad_ref,
    grad_t_ref,
    mass_ref,
    dq_ref,
    keep_ref,
    send_ref,
    acc_ref,
    delta_ref,
    wide_mass_ref,
    prob_ref,
    grad_score_ref,
    bias_ref,
):
    rows = q_ref.shape[0]
    score_scale = 1.0 / math.sqrt(HEAD_WIDTH)
    scale = LOG2_E * score_scale
    place, first, base = window_place(rows)
    starts = starts_ref[0:1, :]
    mass_t = mass_ref[...].T
    for h in range(heads):
        product = grad_ref[:, head(h)].astype(jnp.float32) * att_ref[:, head(h)].astype(jnp.float32)
        delta_ref[h] = jnp.broadcast_to(
            jnp.sum(product, axis=1, keepdims=True), (rows, HEAD_WIDTH)
        )
        wide_mass_ref[h] = jnp.broadcast_to(mass_t[:, h : h + 1], (rows, HEAD_WIDTH))
    chunk = HEAD_WIDTH
    own = BACK * GROUP + place
    begin = begin_ref[0]

    def across(ref, h, piece):
        return jnp.concatenate([ref[h, piece]] * (rows // HEAD_WIDTH), axis=1)

    def visit(block, masked, count=rows):
        keys = win_ref[block, 0]
        keys_t = keys.T
        values_t = values_turned(win_ref, block)
        if masked:
            bias_ref[...] = block_bias(block, base, first, starts).T
        for h in range(heads):
            for at in range(0, count, chunk):
                piece = slice(at, at + chunk)
                scores = (
                    jnp.dot(q_ref[piece, head(h)], keys_t, preferred_element_type=jnp.float32) * scale
                )
                if masked:
                    scores = scores + bias_ref[piece]
                prob = jnp.exp2(scores - across(wide_mass_ref, h, piece))
                prob_ref[h, piece] = prob.astype(jnp.bfloat16)
                grad_prob = jnp.dot(
                    grad_ref[piece, head(h)], values_t, preferred_element_type=jnp.float32
                )
                grad_score_ref[h, piece] = (
                    prob * (grad_prob - across(delta_ref, h, piece))
                ).astype(jnp.bfloat16)
        key_grad = jnp.zeros((HEAD_WIDTH, rows), jnp.float32)
        value_grad = jnp.zeros((HEAD_WIDTH, rows), jnp.float32)
        for h in range(heads):
            value_grad = value_grad + jnp.dot(
                grad_t_ref[h, :, :count], prob_ref[h, :count], preferred_element_type=jnp.float32
            )
        for h in range(heads):
            key_grad = key_grad + jnp.dot(
                qt_ref[h, :, :count], grad_score_ref[h, :count], preferred_element_type=jnp.float32
            )
        for h in range(heads):
            acc_ref[h, :count] += jnp.dot(
                grad_score_ref[h, :count], keys, preferred_element_type=jnp.float32
            )
        give(block, key_grad * score_scale, value_grad)

    def give(block, key_grad, value_grad):
        core, slot = window_slot(block, place)

        @pl.when(core == 0)
        def _():
            keep_ref[slot, 0] = key_grad
            keep_ref[slot, 1] = value_grad

        @pl.when(core == 1)
        def _():
            send_ref[slot, 0] = key_grad.astype(jnp.bfloat16)
            send_ref[slot, 1] = value_grad.astype(jnp.bfloat16)

    def give_nothing(block):
        none = jnp.zeros((HEAD_WIDTH, rows), jnp.float32)
        give(block, none, none)

    acc_ref[...] = jnp.zeros_like(acc_ref)
    pl.loop(0, jnp.where(begin < own, 2, 1))(
        lambda turn: visit(jnp.where(turn == 0, own, begin), True)
    )
    in_first = jnp.where(starts <= jnp.min(starts, axis=1, keepdims=True), 1.0, 0.0)
    in_first = jnp.broadcast_to(in_first, (8, rows)).T[:, 0:1]
    for h in range(heads):
        wide_mass_ref[h] = jnp.where(in_first > 0.5, wide_mass_ref[h], -MASKED)
    few = begin_ref[1] == 1

    @pl.when(few)
    def _():
        pl.loop(begin + 1, own)(lambda block: visit(block, False, rows // 2))

    @pl.when(jnp.logical_not(few))
    def _():
        pl.loop(begin + 1, own)(lambda block: visit(block, False))

    pl.loop(0, begin)(give_nothing)
    pl.loop(own + 1, WINDOW)(give_nothing)
    for h in range(heads):
        dq_ref[:, head(h)] = (acc_ref[h] * score_scale).astype(jnp.bfloat16)


def whole(shape=None):
    return pl.BlockSpec(memory_space=pltpu.VMEM)


SCALARS = pl.BlockSpec(memory_space=pltpu.SMEM)


def attend(prepared, planes, parts, before=()):
    queries_t, starts, begin = prepared
    heads, _, rows = queries_t.shape
    last = len(before) > 0
    visits = len(planes) * GROUP * heads * rows * rows
    sums = [(heads, HEAD_WIDTH + SUM_ROWS, rows), (heads, rows)]
    window = jax.ShapeDtypeStruct((WINDOW, 2, rows, HEAD_WIDTH), jnp.bfloat16)
    working = [
        pltpu.VMEM((heads, rows, rows), jnp.float32),
        pltpu.VMEM((heads, rows, rows), jnp.bfloat16),
        pltpu.VMEM((heads, rows), jnp.float32),
    ]
    if last:
        out_shape = (
            jax.ShapeDtypeStruct((rows, heads * HEAD_WIDTH), jnp.bfloat16),
            jax.ShapeDtypeStruct((heads, rows), jnp.float32),
            window,
        )
        working = [pltpu.VMEM(shape, jnp.float32) for shape in sums] + working
    else:
        out_shape = tuple(jax.ShapeDtypeStruct(shape, jnp.float32) for shape in sums) + (window,)
    return pl.pallas_call(
        partial(forward_kernel, heads, planes, last),
        out_shape=out_shape,
        in_specs=[SCALARS] + [whole()] * (2 + len(parts) + len(before)),
        out_specs=(whole(),) * len(out_shape),
        scratch_shapes=working,
        compiler_params=params(12),
        cost_estimate=pl.CostEstimate(
            flops=4 * visits * HEAD_WIDTH, bytes_accessed=4 * 2**20, transcendentals=visits
        ),
        name="attend",
    )(begin, starts, queries_t, *parts, *before)


def prepare_kernel(lens_ref, wide_ref, out_ref, starts_ref, begin_ref):
    rows = wide_ref.shape[0]
    _, first, base = window_place(rows)
    starts, start, middle = doc_rows(lens_ref, first, rows)
    starts_ref[...] = jnp.broadcast_to(starts, starts_ref.shape)
    begin_ref[0] = (start - base) // rows
    begin_ref[1] = jnp.where(middle > start, 1, 0)
    transpose_heads(wide_ref, out_ref)


def prepare(doc_lengths, queries):
    rows, width = queries.shape
    return pl.pallas_call(
        prepare_kernel,
        out_shape=(
            jax.ShapeDtypeStruct((width // HEAD_WIDTH, HEAD_WIDTH, rows), queries.dtype),
            jax.ShapeDtypeStruct((8, rows), jnp.int32),
            jax.ShapeDtypeStruct((2,), jnp.int32),
        ),
        in_specs=[SCALARS, whole()],
        out_specs=(whole(), whole(), SCALARS),
        compiler_params=params(4),
        name="prepare",
    )(doc_lengths, queries)


def attend_back(prepared, queries, window, attention, grad, grad_t, mass):
    queries_t, starts, begin = prepared
    rows, width = queries.shape
    heads = width // HEAD_WIDTH
    visits = (REACH + 1) * heads * rows * rows
    parts_shape = (2 * PLANES, 2, HEAD_WIDTH, rows)
    return pl.pallas_call(
        partial(backward_kernel, heads),
        out_shape=(
            jax.ShapeDtypeStruct((rows, width), jnp.bfloat16),
            jax.ShapeDtypeStruct(parts_shape, jnp.float32),
            jax.ShapeDtypeStruct(parts_shape, jnp.bfloat16),
        ),
        in_specs=[SCALARS] + [whole()] * 8,
        out_specs=(whole(), whole(), whole()),
        scratch_shapes=[
            pltpu.VMEM((heads, rows, HEAD_WIDTH), jnp.float32),
            pltpu.VMEM((heads, rows, HEAD_WIDTH), jnp.float32),
            pltpu.VMEM((heads, rows, HEAD_WIDTH), jnp.float32),
            pltpu.VMEM((heads, rows, rows), jnp.bfloat16),
            pltpu.VMEM((heads, rows, rows), jnp.bfloat16),
            pltpu.VMEM((rows, rows), jnp.float32),
        ],
        compiler_params=params(16),
        cost_estimate=pl.CostEstimate(
            flops=10 * visits * HEAD_WIDTH, bytes_accessed=8 * 2**20, transcendentals=visits
        ),
        name="attend_back",
    )(begin, starts, queries, queries_t, window, attention, grad, grad_t, mass)


def pair_kernel(keys_ref, values_ref, out_ref):
    out_ref[0] = keys_ref[...]
    turned = values_ref[...].T
    for at in range(0, turned.shape[1], HEAD_WIDTH):
        out_ref[1, at : at + HEAD_WIDTH] = turned[:, at : at + HEAD_WIDTH]


def pair_up(keys, values):
    return pl.pallas_call(
        pair_kernel,
        out_shape=jax.ShapeDtypeStruct((2,) + keys.shape, keys.dtype),
        in_specs=[whole()] * 2,
        out_specs=whole(),
        compiler_params=params(4),
        name="pair_up",
    )(keys, values)


def values_turned(win_ref, block):
    rows = win_ref.shape[2]
    return jnp.concatenate(
        [win_ref[block, 1, at : at + HEAD_WIDTH] for at in range(0, rows, HEAD_WIDTH)], axis=1
    )


def finish_kernel(keep_ref, received_ref, *rest):
    others, outs = rest[:-2], rest[-2:]
    for kind, out_ref in enumerate(outs):
        total = keep_ref[0, kind] + received_ref[0, kind].astype(jnp.float32)
        for other in others:
            total = total + other[kind].astype(jnp.float32)
        out_ref[...] = total.T.astype(jnp.bfloat16)


def finish(keep, received, others):
    _, _, width, rows = keep.shape
    out = jax.ShapeDtypeStruct((rows, width), jnp.bfloat16)
    return pl.pallas_call(
        finish_kernel,
        out_shape=(out, out),
        in_specs=[whole()] * (2 + len(others)),
        out_specs=(whole(), whole()),
        compiler_params=params(4),
        name="finish",
    )(keep, received, *others)


def project_kernel(tile, pieces, half_ref, att_ref, weight_ref, *rest):
    others, outs = rest[: len(rest) - pieces], rest[len(rest) - pieces :]
    columns = weight_ref.shape[1] // 2
    at = 0
    for part in others or outs:
        for there in range(0, part.shape[1], tile):
            piece = pl.ds(pl.multiple_of(half_ref[0] * columns + at, tile), tile)
            total = jnp.dot(
                att_ref[...], weight_ref[:, piece], preferred_element_type=jnp.float32
            ).astype(jnp.bfloat16)
            if others:
                other = part[:, there : there + tile].astype(jnp.float32)
                total = (total.astype(jnp.float32) + other).astype(jnp.bfloat16)
                outs[0][:, at : at + tile] = total
            else:
                part[:, there : there + tile] = total
            at += tile


def project(half, attention, weight, *other, eighths=(8,)):
    rows, depth = attention.shape
    columns = weight.shape[1] // 2
    tile = columns // 8
    pieces = len(eighths)
    shapes = [(rows, columns * part // 8) for part in eighths]
    return pl.pallas_call(
        partial(project_kernel, tile, pieces),
        out_shape=tuple(jax.ShapeDtypeStruct(shape, jnp.bfloat16) for shape in shapes),
        in_specs=[SCALARS] + [whole()] * (2 + len(other)),
        out_specs=(whole(),) * pieces,
        compiler_params=params(8),
        cost_estimate=pl.CostEstimate(
            flops=2 * rows * depth * columns, bytes_accessed=2 * depth * columns, transcendentals=0
        ),
        name="project",
    )(half, attention, weight, *other)


def transpose_heads(wide_ref, out_ref):
    for h in range(out_ref.shape[0]):
        out_ref[h] = wide_ref[:, head(h)].T


def grad_kernel(tile, order_ref, *refs):
    halves, (weight_ref, out_ref, out_t_ref) = refs[:2], refs[2:]
    columns = halves[0].shape[1]
    for at in range(0, weight_ref.shape[0], tile):
        total = 0.0
        for side, cot_ref in enumerate(halves):
            piece = pl.ds(pl.multiple_of(order_ref[side] * columns, columns), columns)
            total += lax.dot_general(
                cot_ref[...], weight_ref[at : at + tile, piece], NT, preferred_element_type=jnp.float32
            )
        out_ref[:, at : at + tile] = total.astype(jnp.bfloat16)
    transpose_heads(out_ref, out_t_ref)


def attention_grad(order, halves, weight, tile=256):
    rows, columns = halves[0].shape
    depth = weight.shape[0]
    return pl.pallas_call(
        partial(grad_kernel, tile),
        out_shape=(
            jax.ShapeDtypeStruct((rows, depth), jnp.bfloat16),
            jax.ShapeDtypeStruct((depth // HEAD_WIDTH, HEAD_WIDTH, rows), jnp.bfloat16),
        ),
        in_specs=[SCALARS] + [whole()] * 3,
        out_specs=(whole(), whole()),
        compiler_params=params(8),
        cost_estimate=pl.CostEstimate(
            flops=4 * rows * depth * columns, bytes_accessed=4 * depth * columns, transcendentals=0
        ),
        name="attention_grad",
    )(order, *halves, weight)


def body(queries, keys, values, out_weight, cotangent, doc_lengths):
    mine = lax.axis_index("tp").astype(jnp.int32).reshape(1)
    theirs = 1 - mine
    order = jnp.concatenate([mine, theirs])
    pair = pair_up(keys, values)
    other_cot = tp_swapped(cotangent)
    planes = [pair] + [sent_on(pair, plane * GROUP) for plane in range(1, PLANES)]
    prepared = prepare(doc_lengths, queries)
    planes[BACK], *prepared = lax.optimization_barrier((planes[BACK], *prepared))

    def group_of(block):
        half = swapped(block, 2)
        return [block, swapped(block, 1), half, swapped(half, 1)]

    def last_group_of(block):
        pairs = [block, swapped(block, 1)]
        return pairs + [swapped(each, 2) for each in pairs]

    groups = [group_of(block) for block in planes[:BACK]] + [last_group_of(planes[BACK])]
    early = tuple(range(BACK))
    sums = attend(prepared, early, sum((groups[plane] for plane in early), []))
    attention, mass, window = attend(prepared, (BACK,), groups[BACK], sums)
    other_terms = project(theirs, attention, out_weight, eighths=(5, 3))
    early_mixed = tp_swapped(other_terms[0])
    other_cot, other_terms = lax.optimization_barrier((other_cot, other_terms))
    grad, grad_t = attention_grad(order, (cotangent, other_cot), out_weight)
    query_grad, keep, send = attend_back(
        prepared, queries, window, attention, grad, grad_t, mass
    )
    send, early_mixed = lax.optimization_barrier((send, early_mixed))
    late_mixed = tp_swapped(other_terms[1])
    received = swapped(send, 1)

    def core_sum(slots):
        return keep[slots] + received[slots].astype(jnp.float32)

    crossed = {}
    for plane in reversed(range(PLANES)):
        crossed[plane] = swapped(core_sum(PLANES + plane).astype(jnp.bfloat16), 2)
    arrived = []
    for plane in range(1, PLANES):
        half_sum = core_sum(plane) + crossed[plane].astype(jnp.float32)
        arrived.append(sent_back(half_sum.astype(jnp.bfloat16), plane * GROUP))
    (mixed_out,) = project(mine, attention, out_weight, early_mixed, late_mixed)
    keys_gradient, values_gradient = finish(keep, received, [crossed[0]] + arrived)
    return (mixed_out, query_grad, keys_gradient, values_gradient)


def solution(mesh):
    in_specs = (P("ctx", "tp"), P("ctx", "tp"), P("ctx", "tp"), P("tp", None), P("ctx", "tp"), P())
    out_specs = (P("ctx", "tp"), P("ctx", "tp"), P("ctx", "tp"), P("ctx", "tp"))
    return jax.shard_map(body, mesh=mesh, in_specs=in_specs, out_specs=out_specs, check_vma=False)
```

```python
from functools import partial
import math

import jax
import jax.numpy as jnp
from jax import lax
from jax.experimental import pallas as pl
from jax.experimental.pallas import tpu as pltpu
from jax.sharding import PartitionSpec as P

HEAD_WIDTH = 128
REACH = 8
GROUP = 4
BACK = REACH // GROUP
PLANES = BACK + 1
WINDOW = PLANES * GROUP
LOG2_E = math.log2(math.e)
MASKED = -1e30
EXCESS = 64.0
SUM_ROWS = 16
NT = (((1,), (1,)), ((), ()))


def sent_on(block, distance):
    size = lax.axis_size("ctx")
    return lax.ppermute(block, "ctx", [(i, i + distance) for i in range(size - distance)])


def sent_back(block, distance):
    size = lax.axis_size("ctx")
    return lax.ppermute(block, "ctx", [(i, (i - distance) % size) for i in range(size)])


def swapped(block, bit):
    return lax.ppermute(block, "ctx", [(i, i ^ bit) for i in range(lax.axis_size("ctx"))])


def tp_swapped(block):
    return lax.ppermute(block, "tp", [(0, 1), (1, 0)])


def params(mebibytes):
    return pltpu.CompilerParams(vmem_limit_bytes=mebibytes * 2**20)


def window_slot(block, place):
    plane = BACK - block // GROUP
    half = (block // 2 + place // 2) % 2
    core = (block + place) % 2
    return core, half * PLANES + plane


def doc_rows(lens_ref, first, rows):
    positions = first + lax.broadcasted_iota(jnp.int32, (1, rows), 1)

    def add_doc(doc, carry):
        end, starts, start, middle = carry
        length = lens_ref[doc]
        end = end + length
        return (
            end,
            starts + jnp.where(positions >= end, length, 0),
            start + jnp.where(first >= end, length, 0),
            middle + jnp.where(first + rows // 2 >= end, length, 0),
        )

    zero = jnp.int32(0)
    _, starts, start, middle = lax.fori_loop(
        0, lens_ref.shape[0], add_doc, (zero, jnp.zeros((1, rows), jnp.int32), zero, zero)
    )
    return starts, start, middle


def block_bias(block, base, first, starts):
    rows = starts.shape[1]
    key_pos = base + block * rows + lax.broadcasted_iota(jnp.int32, (rows, rows), 0)
    positions = first + lax.broadcasted_iota(jnp.int32, (1, rows), 1)
    return jnp.where((key_pos >= starts) & (key_pos <= positions), 0.0, MASKED).astype(jnp.float32)


def head(h):
    return slice(h * HEAD_WIDTH, (h + 1) * HEAD_WIDTH)


def window_place(rows):
    device = lax.axis_index("ctx")
    place = device % GROUP
    first = device * rows
    base = first - (BACK * GROUP + place) * rows
    return place, first, base


def forward_kernel(heads, planes, last, begin_ref, starts_ref, qt_ref, *rest):
    count = len(planes) * GROUP
    parts, rest = rest[:count], rest[count:]
    if last:
        acc_in, shift_in, win_in = rest[:3]
        out_ref, mass_ref, win_ref, acc_ref, shift_ref, score_ref, prob_ref, most_ref = rest[3:]
    else:
        acc_ref, shift_ref, win_ref, score_ref, prob_ref, most_ref = rest
    rows = qt_ref.shape[2]
    scale = LOG2_E / math.sqrt(HEAD_WIDTH)
    place, first, base = window_place(rows)
    begin = begin_ref[0]
    own = BACK * GROUP + place
    starts = starts_ref[0:1, :]
    in_first = starts <= jnp.min(starts, axis=1, keepdims=True)
    for at, plane in enumerate(planes):
        for way in range(GROUP):
            where = (BACK - plane) * GROUP + (place ^ way)
            win_ref[where] = parts[at * GROUP + way][...]
    if last:
        kept = (BACK + 1 - planes[0]) * GROUP
        win_ref[kept:] = win_in[kept:]

    def values_of(block):
        ones = jnp.ones((SUM_ROWS, rows), jnp.bfloat16)
        return jnp.concatenate([values_turned(win_ref, block), ones], axis=0)

    def weigh(values_t, h):
        return jnp.dot(values_t, prob_ref[h], preferred_element_type=jnp.float32)

    def visit_own():
        keys, values_t = win_ref[own, 0], values_of(own)
        bias = block_bias(own, base, first, starts)
        for h in range(heads):
            score_ref[h] = jnp.dot(keys, qt_ref[h], preferred_element_type=jnp.float32)
        for h in range(heads):
            scores = score_ref[h] * scale + bias
            shift = jnp.max(scores, axis=0, keepdims=True)
            shift_ref[h : h + 1, :] = shift
            prob_ref[h] = jnp.exp2(scores - shift).astype(jnp.bfloat16)
        for h in range(heads):
            acc_ref[h] = weigh(values_t, h)

    def visit(block, masked):
        keys, values_t = win_ref[block, 0], values_of(block)
        if masked:
            bias = block_bias(block, base, first, starts)
        for h in range(heads):
            shift = jnp.where(in_first, shift_ref[h : h + 1, :], -MASKED)
            scores = jnp.dot(keys, qt_ref[h], preferred_element_type=jnp.float32) * scale - shift
            if masked:
                scores = scores + bias
            most_ref[h : h + 1, :] = jnp.maximum(
                most_ref[h : h + 1, :], jnp.max(scores, axis=0, keepdims=True)
            )
            prob_ref[h] = jnp.exp2(scores).astype(jnp.bfloat16)
        for h in range(heads):
            acc_ref[h] += weigh(values_t, h)

    def visit_following(block):
        keys, values_t = win_ref[block, 0], values_of(block)
        bias = block_bias(block, base, first, starts)
        for h in range(heads):
            score_ref[h] = jnp.dot(keys, qt_ref[h], preferred_element_type=jnp.float32)
        for h in range(heads):
            scores = score_ref[h] * scale + bias
            old_shift = shift_ref[h : h + 1, :]
            shift = jnp.maximum(old_shift, jnp.max(scores, axis=0, keepdims=True))
            shift_ref[h : h + 1, :] = shift
            prob_ref[h] = jnp.exp2(scores - shift).astype(jnp.bfloat16)
            acc_ref[h] = acc_ref[h] * jnp.exp2(old_shift - shift)
        for h in range(heads):
            acc_ref[h] += weigh(values_t, h)

    lowest = (BACK - planes[-1]) * GROUP
    end = jnp.minimum(own, (BACK - planes[0] + 1) * GROUP)

    def begin_sums():
        if last:
            acc_ref[...] = acc_in[...]
            shift_ref[...] = shift_in[...]
        else:
            visit_own()

    begin_sums()
    most_ref[...] = jnp.full_like(most_ref, MASKED)

    @pl.when((begin >= lowest) & (begin < end))
    def _():
        visit(begin, True)

    pl.loop(jnp.maximum(begin + 1, lowest), end)(lambda block: visit(block, False))

    @pl.when(jnp.max(most_ref[...]) > EXCESS)
    def _():
        begin_sums()
        pl.loop(jnp.maximum(begin, lowest), end)(visit_following)

    if last:
        for h in range(heads):
            total = acc_ref[h, HEAD_WIDTH : HEAD_WIDTH + 1, :]
            mass_ref[h : h + 1, :] = shift_ref[h : h + 1, :] + jnp.log2(total)
            out_ref[:, head(h)] = (acc_ref[h, :HEAD_WIDTH] / total).T.astype(jnp.bfloat16)


def backward_kernel(
    heads,
    begin_ref,
    starts_ref,
    q_ref,
    qt_ref,
    win_ref,
    att_ref,
    grad_ref,
    grad_t_ref,
    mass_ref,
    dq_ref,
    keep_ref,
    send_ref,
    acc_ref,
    delta_ref,
    wide_mass_ref,
    prob_ref,
    grad_score_ref,
    bias_ref,
):
    rows = q_ref.shape[0]
    score_scale = 1.0 / math.sqrt(HEAD_WIDTH)
    scale = LOG2_E * score_scale
    place, first, base = window_place(rows)
    starts = starts_ref[0:1, :]
    mass_t = mass_ref[...].T
    for h in range(heads):
        product = grad_ref[:, head(h)].astype(jnp.float32) * att_ref[:, head(h)].astype(jnp.float32)
        delta_ref[h] = jnp.broadcast_to(
            jnp.sum(product, axis=1, keepdims=True), (rows, HEAD_WIDTH)
        )
        wide_mass_ref[h] = jnp.broadcast_to(mass_t[:, h : h + 1], (rows, HEAD_WIDTH))
    chunk = HEAD_WIDTH
    own = BACK * GROUP + place
    begin = begin_ref[0]

    def across(ref, h, piece):
        return jnp.concatenate([ref[h, piece]] * (rows // HEAD_WIDTH), axis=1)

    def visit(block, masked, count=rows):
        keys = win_ref[block, 0]
        keys_t = keys.T
        values_t = values_turned(win_ref, block)
        if masked:
            bias_ref[...] = block_bias(block, base, first, starts).T
        for h in range(heads):
            for at in range(0, count, chunk):
                piece = slice(at, at + chunk)
                scores = (
                    jnp.dot(q_ref[piece, head(h)], keys_t, preferred_element_type=jnp.float32) * scale
                )
                if masked:
                    scores = scores + bias_ref[piece]
                prob = jnp.exp2(scores - across(wide_mass_ref, h, piece))
                prob_ref[h, piece] = prob.astype(jnp.bfloat16)
                grad_prob = jnp.dot(
                    grad_ref[piece, head(h)], values_t, preferred_element_type=jnp.float32
                )
                grad_score_ref[h, piece] = (
                    prob * (grad_prob - across(delta_ref, h, piece))
                ).astype(jnp.bfloat16)
        key_grad = jnp.zeros((HEAD_WIDTH, rows), jnp.float32)
        value_grad = jnp.zeros((HEAD_WIDTH, rows), jnp.float32)
        for h in range(heads):
            value_grad = value_grad + jnp.dot(
                grad_t_ref[h, :, :count], prob_ref[h, :count], preferred_element_type=jnp.float32
            )
        for h in range(heads):
            key_grad = key_grad + jnp.dot(
                qt_ref[h, :, :count], grad_score_ref[h, :count], preferred_element_type=jnp.float32
            )
        for h in range(heads):
            acc_ref[h, :count] += jnp.dot(
                grad_score_ref[h, :count], keys, preferred_element_type=jnp.float32
            )
        give(block, key_grad * score_scale, value_grad)

    def give(block, key_grad, value_grad):
        core, slot = window_slot(block, place)

        @pl.when(core == 0)
        def _():
            keep_ref[slot, 0] = key_grad
            keep_ref[slot, 1] = value_grad

        @pl.when(core == 1)
        def _():
            send_ref[slot, 0] = key_grad.astype(jnp.bfloat16)
            send_ref[slot, 1] = value_grad.astype(jnp.bfloat16)

    def give_nothing(block):
        none = jnp.zeros((HEAD_WIDTH, rows), jnp.float32)
        give(block, none, none)

    acc_ref[...] = jnp.zeros_like(acc_ref)
    pl.loop(0, jnp.where(begin < own, 2, 1))(
        lambda turn: visit(jnp.where(turn == 0, own, begin), True)
    )
    in_first = jnp.where(starts <= jnp.min(starts, axis=1, keepdims=True), 1.0, 0.0)
    in_first = jnp.broadcast_to(in_first, (8, rows)).T[:, 0:1]
    for h in range(heads):
        wide_mass_ref[h] = jnp.where(in_first > 0.5, wide_mass_ref[h], -MASKED)
    few = begin_ref[1] == 1

    @pl.when(few)
    def _():
        pl.loop(begin + 1, own)(lambda block: visit(block, False, rows // 2))

    @pl.when(jnp.logical_not(few))
    def _():
        pl.loop(begin + 1, own)(lambda block: visit(block, False))

    pl.loop(0, begin)(give_nothing)
    pl.loop(own + 1, WINDOW)(give_nothing)
    for h in range(heads):
        dq_ref[:, head(h)] = (acc_ref[h] * score_scale).astype(jnp.bfloat16)


def whole(shape=None):
    return pl.BlockSpec(memory_space=pltpu.VMEM)


SCALARS = pl.BlockSpec(memory_space=pltpu.SMEM)


def attend(prepared, planes, parts, before=()):
    queries_t, starts, begin = prepared
    heads, _, rows = queries_t.shape
    last = len(before) > 0
    visits = len(planes) * GROUP * heads * rows * rows
    sums = [(heads, HEAD_WIDTH + SUM_ROWS, rows), (heads, rows)]
    window = jax.ShapeDtypeStruct((WINDOW, 2, rows, HEAD_WIDTH), jnp.bfloat16)
    working = [
        pltpu.VMEM((heads, rows, rows), jnp.float32),
        pltpu.VMEM((heads, rows, rows), jnp.bfloat16),
        pltpu.VMEM((heads, rows), jnp.float32),
    ]
    if last:
        out_shape = (
            jax.ShapeDtypeStruct((rows, heads * HEAD_WIDTH), jnp.bfloat16),
            jax.ShapeDtypeStruct((heads, rows), jnp.float32),
            window,
        )
        working = [pltpu.VMEM(shape, jnp.float32) for shape in sums] + working
    else:
        out_shape = tuple(jax.ShapeDtypeStruct(shape, jnp.float32) for shape in sums) + (window,)
    return pl.pallas_call(
        partial(forward_kernel, heads, planes, last),
        out_shape=out_shape,
        in_specs=[SCALARS] + [whole()] * (2 + len(parts) + len(before)),
        out_specs=(whole(),) * len(out_shape),
        scratch_shapes=working,
        compiler_params=params(12),
        cost_estimate=pl.CostEstimate(
            flops=4 * visits * HEAD_WIDTH, bytes_accessed=4 * 2**20, transcendentals=visits
        ),
        name="attend",
    )(begin, starts, queries_t, *parts, *before)


def prepare_kernel(lens_ref, wide_ref, out_ref, starts_ref, begin_ref):
    rows = wide_ref.shape[0]
    _, first, base = window_place(rows)
    starts, start, middle = doc_rows(lens_ref, first, rows)
    starts_ref[...] = jnp.broadcast_to(starts, starts_ref.shape)
    begin_ref[0] = (start - base) // rows
    begin_ref[1] = jnp.where(middle > start, 1, 0)
    transpose_heads(wide_ref, out_ref)


def prepare(doc_lengths, queries):
    rows, width = queries.shape
    return pl.pallas_call(
        prepare_kernel,
        out_shape=(
            jax.ShapeDtypeStruct((width // HEAD_WIDTH, HEAD_WIDTH, rows), queries.dtype),
            jax.ShapeDtypeStruct((8, rows), jnp.int32),
            jax.ShapeDtypeStruct((2,), jnp.int32),
        ),
        in_specs=[SCALARS, whole()],
        out_specs=(whole(), whole(), SCALARS),
        compiler_params=params(4),
        name="prepare",
    )(doc_lengths, queries)


def attend_back(prepared, queries, window, attention, grad, grad_t, mass):
    queries_t, starts, begin = prepared
    rows, width = queries.shape
    heads = width // HEAD_WIDTH
    visits = (REACH + 1) * heads * rows * rows
    parts_shape = (2 * PLANES, 2, HEAD_WIDTH, rows)
    return pl.pallas_call(
        partial(backward_kernel, heads),
        out_shape=(
            jax.ShapeDtypeStruct((rows, width), jnp.bfloat16),
            jax.ShapeDtypeStruct(parts_shape, jnp.float32),
            jax.ShapeDtypeStruct(parts_shape, jnp.bfloat16),
        ),
        in_specs=[SCALARS] + [whole()] * 8,
        out_specs=(whole(), whole(), whole()),
        scratch_shapes=[
            pltpu.VMEM((heads, rows, HEAD_WIDTH), jnp.float32),
            pltpu.VMEM((heads, rows, HEAD_WIDTH), jnp.float32),
            pltpu.VMEM((heads, rows, HEAD_WIDTH), jnp.float32),
            pltpu.VMEM((heads, rows, rows), jnp.bfloat16),
            pltpu.VMEM((heads, rows, rows), jnp.bfloat16),
            pltpu.VMEM((rows, rows), jnp.float32),
        ],
        compiler_params=params(16),
        cost_estimate=pl.CostEstimate(
            flops=10 * visits * HEAD_WIDTH, bytes_accessed=8 * 2**20, transcendentals=visits
        ),
        name="attend_back",
    )(begin, starts, queries, queries_t, window, attention, grad, grad_t, mass)


def pair_kernel(keys_ref, values_ref, out_ref):
    out_ref[0] = keys_ref[...]
    turned = values_ref[...].T
    for at in range(0, turned.shape[1], HEAD_WIDTH):
        out_ref[1, at : at + HEAD_WIDTH] = turned[:, at : at + HEAD_WIDTH]


def pair_up(keys, values):
    return pl.pallas_call(
        pair_kernel,
        out_shape=jax.ShapeDtypeStruct((2,) + keys.shape, keys.dtype),
        in_specs=[whole()] * 2,
        out_specs=whole(),
        compiler_params=params(4),
        name="pair_up",
    )(keys, values)


def values_turned(win_ref, block):
    rows = win_ref.shape[2]
    return jnp.concatenate(
        [win_ref[block, 1, at : at + HEAD_WIDTH] for at in range(0, rows, HEAD_WIDTH)], axis=1
    )


def finish_kernel(keep_ref, received_ref, *rest):
    others, outs = rest[:-2], rest[-2:]
    for kind, out_ref in enumerate(outs):
        total = keep_ref[0, kind] + received_ref[0, kind].astype(jnp.float32)
        for other in others:
            total = total + other[kind].astype(jnp.float32)
        out_ref[...] = total.T.astype(jnp.bfloat16)


def finish(keep, received, others):
    _, _, width, rows = keep.shape
    out = jax.ShapeDtypeStruct((rows, width), jnp.bfloat16)
    return pl.pallas_call(
        finish_kernel,
        out_shape=(out, out),
        in_specs=[whole()] * (2 + len(others)),
        out_specs=(whole(), whole()),
        compiler_params=params(4),
        name="finish",
    )(keep, received, *others)


def project_kernel(tile, pieces, half_ref, att_ref, weight_ref, *rest):
    others, outs = rest[: len(rest) - pieces], rest[len(rest) - pieces :]
    columns = weight_ref.shape[1] // 2
    at = 0
    for part in others or outs:
        for there in range(0, part.shape[1], tile):
            piece = pl.ds(pl.multiple_of(half_ref[0] * columns + at, tile), tile)
            total = jnp.dot(
                att_ref[...], weight_ref[:, piece], preferred_element_type=jnp.float32
            ).astype(jnp.bfloat16)
            if others:
                other = part[:, there : there + tile].astype(jnp.float32)
                total = (total.astype(jnp.float32) + other).astype(jnp.bfloat16)
                outs[0][:, at : at + tile] = total
            else:
                part[:, there : there + tile] = total
            at += tile


def project(half, attention, weight, *other, eighths=(8,)):
    rows, depth = attention.shape
    columns = weight.shape[1] // 2
    tile = columns // 8
    pieces = len(eighths)
    shapes = [(rows, columns * part // 8) for part in eighths]
    return pl.pallas_call(
        partial(project_kernel, tile, pieces),
        out_shape=tuple(jax.ShapeDtypeStruct(shape, jnp.bfloat16) for shape in shapes),
        in_specs=[SCALARS] + [whole()] * (2 + len(other)),
        out_specs=(whole(),) * pieces,
        compiler_params=params(8),
        cost_estimate=pl.CostEstimate(
            flops=2 * rows * depth * columns, bytes_accessed=2 * depth * columns, transcendentals=0
        ),
        name="project",
    )(half, attention, weight, *other)


def transpose_heads(wide_ref, out_ref):
    for h in range(out_ref.shape[0]):
        out_ref[h] = wide_ref[:, head(h)].T


def grad_kernel(tile, order_ref, *refs):
    halves, (weight_ref, out_ref, out_t_ref) = refs[:2], refs[2:]
    columns = halves[0].shape[1]
    for at in range(0, weight_ref.shape[0], tile):
        total = 0.0
        for side, cot_ref in enumerate(halves):
            piece = pl.ds(pl.multiple_of(order_ref[side] * columns, columns), columns)
            total += lax.dot_general(
                cot_ref[...], weight_ref[at : at + tile, piece], NT, preferred_element_type=jnp.float32
            )
        out_ref[:, at : at + tile] = total.astype(jnp.bfloat16)
    transpose_heads(out_ref, out_t_ref)


def attention_grad(order, halves, weight, tile=256):
    rows, columns = halves[0].shape
    depth = weight.shape[0]
    return pl.pallas_call(
        partial(grad_kernel, tile),
        out_shape=(
            jax.ShapeDtypeStruct((rows, depth), jnp.bfloat16),
            jax.ShapeDtypeStruct((depth // HEAD_WIDTH, HEAD_WIDTH, rows), jnp.bfloat16),
        ),
        in_specs=[SCALARS] + [whole()] * 3,
        out_specs=(whole(), whole()),
        compiler_params=params(8),
        cost_estimate=pl.CostEstimate(
            flops=4 * rows * depth * columns, bytes_accessed=4 * depth * columns, transcendentals=0
        ),
        name="attention_grad",
    )(order, *halves, weight)


def body(queries, keys, values, out_weight, cotangent, doc_lengths):
    mine = lax.axis_index("tp").astype(jnp.int32).reshape(1)
    theirs = 1 - mine
    order = jnp.concatenate([mine, theirs])
    pair = pair_up(keys, values)
    other_cot = tp_swapped(cotangent)
    planes = [pair] + [sent_on(pair, plane * GROUP) for plane in range(1, PLANES)]
    prepared = prepare(doc_lengths, queries)
    planes[BACK], *prepared = lax.optimization_barrier((planes[BACK], *prepared))

    def group_of(block):
        half = swapped(block, 2)
        return [block, swapped(block, 1), half, swapped(half, 1)]

    def last_group_of(block):
        pairs = [block, swapped(block, 1)]
        return pairs + [swapped(each, 2) for each in pairs]

    groups = [group_of(block) for block in planes[:BACK]] + [last_group_of(planes[BACK])]
    early = tuple(range(BACK))
    sums = attend(prepared, early, sum((groups[plane] for plane in early), []))
    attention, mass, window = attend(prepared, (BACK,), groups[BACK], sums)
    other_terms = project(theirs, attention, out_weight, eighths=(5, 3))
    early_mixed = tp_swapped(other_terms[0])
    other_cot, other_terms = lax.optimization_barrier((other_cot, other_terms))
    grad, grad_t = attention_grad(order, (cotangent, other_cot), out_weight)
    query_grad, keep, send = attend_back(
        prepared, queries, window, attention, grad, grad_t, mass
    )
    send, early_mixed = lax.optimization_barrier((send, early_mixed))
    late_mixed = tp_swapped(other_terms[1])
    received = swapped(send, 1)

    def core_sum(slots):
        return keep[slots] + received[slots].astype(jnp.float32)

    crossing = [core_sum(PLANES + plane).astype(jnp.bfloat16) for plane in range(PLANES)]
    crossed = [None] + [swapped(block, 2) for block in crossing[1:]]
    crossed[1], crossing[0] = lax.optimization_barrier((crossed[1], crossing[0]))
    crossed[0] = swapped(crossing[0], 2)
    arrived = []
    for plane in range(1, PLANES):
        half_sum = core_sum(plane) + crossed[plane].astype(jnp.float32)
        arrived.append(sent_back(half_sum.astype(jnp.bfloat16), plane * GROUP))
    (mixed_out,) = project(mine, attention, out_weight, early_mixed, late_mixed)
    keys_gradient, values_gradient = finish(keep, received, [crossed[0]] + arrived)
    return (mixed_out, query_grad, keys_gradient, values_gradient)


def solution(mesh):
    in_specs = (P("ctx", "tp"), P("ctx", "tp"), P("ctx", "tp"), P("tp", None), P("ctx", "tp"), P())
    out_specs = (P("ctx", "tp"), P("ctx", "tp"), P("ctx", "tp"), P("ctx", "tp"))
    return jax.shard_map(body, mesh=mesh, in_specs=in_specs, out_specs=out_specs, check_vma=False)
```
